128 devices in a mesh: seq: 16 (over z, x), batch: 8 (over y, core).
Axes of the slice: x: 4, y: 4, z: 4, core: 2. Of those that a mesh axis runs over, the one named last changes fastest.
Arguments:
- tokens: bfloat16 [16, 2048, 576], P('batch', 'seq'), may hold values from -6 to 6
- doc_lengths: int32 [16, 16], P('batch'), may hold values from 0 to 2048, as said below
- second_query: bfloat16 [16, 2048, 576], P('batch', 'seq'), may hold values from -6 to 6
- second_grad: bfloat16 [16, 2048, 576], P('batch', 'seq'), may hold values from -6 to 6
- out_grad: bfloat16 [16, 2048, 576], P('batch', 'seq'), may hold values from -6 to 6
- first_gain: bfloat16 [576], replicated, may hold values from 0.5 to 1.5
- query_weight: bfloat16 [576, 576], replicated, may hold values from -0.25 to 0.25
- key_weight: bfloat16 [576, 192], replicated, may hold values from -0.25 to 0.25
- value_weight: bfloat16 [576, 192], replicated, may hold values from -0.25 to 0.25
- output_weight: bfloat16 [576, 576], replicated, may hold values from -1 to 1
- second_gain: bfloat16 [576], replicated, may hold values from 0.5 to 1.5
- gate_weight: bfloat16 [576, 1536], replicated, may hold values from -0.25 to 0.25
- up_weight: bfloat16 [576, 1536], replicated, may hold values from -0.25 to 0.25
- down_weight: bfloat16 [1536, 576], replicated, may hold values from -0.15625 to 0.15625
Outputs:
- result: bfloat16 [16, 2048, 576], P('batch', 'seq')
- input_grad: bfloat16 [16, 2048, 576], P('batch', 'seq')
- second_query_grad: bfloat16 [16, 2048, 576], P('batch', 'seq')
- first_gain_grad: float32 [576], replicated
- query_weight_grad: float32 [576, 576], replicated
- key_weight_grad: float32 [576, 192], replicated
- value_weight_grad: float32 [576, 192], replicated
- output_weight_grad: float32 [576, 576], replicated
- second_gain_grad: float32 [576], replicated
- gate_weight_grad: float32 [576, 1536], replicated
- up_weight_grad: float32 [576, 1536], replicated
- down_weight_grad: float32 [1536, 576], replicated
The draws below stay inside these ranges and needn't reach their ends.
Inputs may be any that keep to these rules, and one draw needn't show every extreme that they name: `doc_lengths`: each row sums to 2048. Of the 2 sequences that one index of batch holds, one, chosen by the seed, is a single document of 2048 tokens and the other entries of its row are 0.
All inputs are finite; a program needn't handle non-finite values.
Results may differ from the reference program's by a relative error of at most 0.015.
Values may be sent and summed in bfloat16 or wider, within the bound.
No kernel may reach another device: no remote copies, remote signals or barrier semaphores. Data moves between devices by JAX's collectives and lax.ppermute only.
A program may use at most 128 MiB of HBM per device.

```python
import math
import jax
import jax.numpy as jnp
from jax import lax

D = 576
HEADS = 9
KVH = 3
HD = 64
FF = 1536
MB = 2
NDOC = 16
QW = 576
KW = 192
SEQ_LEN = 2048
SEQS = 16


def draw_doc_lengths(key, part):
    key = jax.random.fold_in(key, 7)
    key_one, key_two, key_three = jax.random.split(key, 3)
    shares = jax.random.randint(key_one, (SEQS, NDOC), 1, 9).astype(jnp.int32)
    share_total = jnp.sum(shares, axis=1, keepdims=True).astype(jnp.int32)
    spread = (shares * SEQ_LEN // share_total).astype(jnp.int32)
    places = lax.iota(jnp.int32, NDOC)
    remainder = (SEQ_LEN - jnp.sum(spread, axis=1, keepdims=True)).astype(jnp.int32)
    spread = spread + remainder * (places == NDOC - 1)[None, :].astype(jnp.int32)
    chosen = jax.random.randint(key_two, (SEQS // MB, 1), 0, MB).astype(jnp.int32)
    member = (lax.iota(jnp.int32, MB)[None, :] == chosen).reshape(SEQS, 1)
    single = jax.random.randint(key_three, (SEQS, 1), 0, NDOC).astype(jnp.int32)
    single_doc = SEQ_LEN * (places[None, :] == single).astype(jnp.int32)
    return jnp.where(member, single_doc, spread).astype(jnp.int32)


def level_of(key, shape, shards, least, top_value):
    def one(dim, parts):
        heights = jax.random.uniform(jax.random.fold_in(jax.random.fold_in(key, 6), dim), (parts,), jnp.float32, least / len(shards), top_value / len(shards))
        return jnp.repeat(jnp.exp(heights), shape[dim] // parts).reshape((-1,) + (1,) * (len(shape) - dim - 1))

    level = one(*shards[0])
    for cut in shards[1:]:
        level = level * one(*cut)
    return level


def gaussian(rng, dims, scale, limit, pieces=(), held_as=jnp.bfloat16):
    drawn = scale * jax.random.normal(rng, dims, jnp.float32)
    if pieces:
        drawn = drawn * level_of(rng, dims, pieces, -0.22, 0.18)
    return jnp.clip(drawn, -limit, limit).astype(held_as)


def setup_inputs(seed: int = 0) -> dict:
    keys = jax.random.split(jax.random.key(seed), 15)
    tokens = gaussian(keys[0], (SEQS, SEQ_LEN, D), 1.0, 6.0, ((0, 8), (1, 16)))
    doc_lengths = draw_doc_lengths(jax.random.fold_in(keys[14], 71), 0)
    second_query = gaussian(keys[2], (SEQS, SEQ_LEN, QW), 1.0, 6.0, ((0, 8), (1, 16)))
    second_grad = gaussian(keys[3], (SEQS, SEQ_LEN, QW), 1.0, 6.0, ((0, 8), (1, 16)))
    out_grad = gaussian(keys[4], (SEQS, SEQ_LEN, D), 1.0, 6.0, ((0, 8), (1, 16)))
    first_gain = jnp.clip(1.0 + 0.1 * jax.random.normal(keys[5], (D,), jnp.float32), 0.5, 1.5).astype(jnp.bfloat16)
    query_weight = gaussian(keys[6], (D, QW), D ** -0.5, 0.25)
    key_weight = gaussian(keys[7], (D, KW), D ** -0.5, 0.25)
    value_weight = gaussian(keys[8], (D, KW), D ** -0.5, 0.25)
    output_weight = gaussian(keys[9], (QW, D), (QW // 16) ** -0.5, 1.0)
    second_gain = jnp.clip(1.0 + 0.1 * jax.random.normal(keys[10], (D,), jnp.float32), 0.5, 1.5).astype(jnp.bfloat16)
    gate_weight = gaussian(keys[11], (D, FF), D ** -0.5, 0.25)
    up_weight = gaussian(keys[12], (D, FF), D ** -0.5, 0.25)
    down_weight = gaussian(keys[13], (FF, D), FF ** -0.5, 0.15625)
    return dict(tokens=tokens, doc_lengths=doc_lengths, second_query=second_query, second_grad=second_grad, out_grad=out_grad, first_gain=first_gain, query_weight=query_weight, key_weight=key_weight, value_weight=value_weight, output_weight=output_weight, second_gain=second_gain, gate_weight=gate_weight, up_weight=up_weight, down_weight=down_weight)


NEGATIVE = -1e+30
EPSILON = 1e-05
ROPE_BASE = 100000.0
PRECISE = lax.Precision.HIGHEST

@jax.custom_vjp
def low(v):
    return lax.optimization_barrier(v.astype(jnp.bfloat16)).astype(jnp.float32)

@jax.custom_vjp
def low_back(v):
    return v

def low_keep(v):
    return (low(v), None)

def low_pass(kept, grad):
    return (grad,)

def back_keep(v):
    return (v, None)

def back_low(kept, grad):
    return (low(grad),)
low.defvjp(low_keep, low_pass)
low_back.defvjp(back_keep, back_low)

def doc_tables(lengths, seq_total):
    doc_ends = jnp.cumsum(lengths).astype(jnp.int32)
    places = lax.iota(jnp.int32, seq_total)
    passed = (doc_ends[None, :] <= places[:, None]).astype(jnp.int32)
    segment = lax.optimization_barrier(jnp.sum(passed, axis=1)).astype(jnp.int32)
    doc_start = lax.optimization_barrier(jnp.sum(passed * lengths[None, :], axis=1)).astype(jnp.int32)
    return (segment, (places - doc_start).astype(jnp.int32))

def rope_tables(position, head_width):
    half_width = head_width // 2
    frequency = ROPE_BASE ** (-(lax.iota(jnp.float32, half_width) * 2.0) / head_width)
    angles = position.astype(jnp.float32)[:, None] * frequency[None, :]
    return (jnp.cos(angles), jnp.sin(angles))

def rotate(vector, cosine_table, sine_table):
    half_width = vector.shape[-1] // 2
    front_half = vector[..., :half_width]
    back_half = vector[..., half_width:]
    cosine = cosine_table[:, None, :]
    sine_part = sine_table[:, None, :]
    return jnp.concatenate([front_half * cosine - back_half * sine_part, back_half * cosine + front_half * sine_part], axis=-1)

def normalize(vector, gain_vec):
    return vector * lax.rsqrt(lax.optimization_barrier(jnp.mean(vector * vector, axis=-1, keepdims=True)) + EPSILON) * gain_vec

def attend(query, second, key, value, segment):
    seq_total = query.shape[0]
    group_size = HEADS // KVH
    joined = jnp.concatenate([query.reshape(seq_total, KVH, group_size, HD), second.reshape(seq_total, KVH, group_size, HD)], axis=2)
    all_keys = key.reshape(seq_total, KVH, HD)
    all_values = value.reshape(seq_total, KVH, HD)
    places = lax.iota(jnp.int32, seq_total)
    visible = (segment[None, :] == segment[:, None]) & (places[None, :] <= places[:, None])
    scores = low_back(jnp.einsum('tkgd,skd->kgts', joined, all_keys, precision=PRECISE) * (1.0 / math.sqrt(HD)))
    masked = jnp.where(visible[None, None], scores, NEGATIVE)
    probability = low(jax.nn.softmax(masked, axis=-1))
    attended = jnp.einsum('kgts,skd->tkgd', probability, all_values, precision=PRECISE)
    return (attended[:, :, :group_size].reshape(seq_total, HEADS * HD), attended[:, :, group_size:].reshape(seq_total, HEADS * HD))

def one_layer(inputs, second, lengths, first_gain, query_weight, key_weight, value_weight, output_weight, second_gain, gate_weight, up_weight, down_weight):
    seq_total = inputs.shape[0]
    segment, position = doc_tables(lengths, seq_total)
    cosine_table, sine_table = rope_tables(position, HD)
    normed = low(normalize(inputs, first_gain))
    query_pre = low_back(jnp.dot(normed, query_weight, precision=PRECISE, preferred_element_type=jnp.float32))
    key_pre = low_back(jnp.dot(normed, key_weight, precision=PRECISE, preferred_element_type=jnp.float32))
    value_pre = jnp.dot(normed, value_weight, precision=PRECISE, preferred_element_type=jnp.float32)
    query = low(rotate(query_pre.reshape(seq_total, HEADS, HD), cosine_table, sine_table)).reshape(seq_total, HEADS * HD)
    key = low(rotate(key_pre.reshape(seq_total, KVH, HD), cosine_table, sine_table)).reshape(seq_total, KVH * HD)
    value = low(low_back(value_pre))
    first_out, second_out = attend(query, second, key, value, segment)
    first_out = low(low_back(first_out))
    middle = inputs + low_back(jnp.dot(first_out, output_weight, precision=PRECISE, preferred_element_type=jnp.float32))
    normed_two = low(normalize(middle, second_gain))
    gate_pre = low_back(jnp.dot(normed_two, gate_weight, precision=PRECISE, preferred_element_type=jnp.float32))
    up_pre = low_back(jnp.dot(normed_two, up_weight, precision=PRECISE, preferred_element_type=jnp.float32))
    hidden = low(jax.nn.silu(gate_pre) * up_pre)
    output = middle + low_back(jnp.dot(hidden, down_weight, precision=PRECISE, preferred_element_type=jnp.float32))
    return (output, second_out)

def reference(tokens, doc_lengths, second_query, second_grad, out_grad, first_gain, query_weight, key_weight, value_weight, output_weight, second_gain, gate_weight, up_weight, down_weight):
    float_weights = tuple((weight.astype(jnp.float32) for weight in (first_gain, query_weight, key_weight, value_weight, output_weight, second_gain, gate_weight, up_weight, down_weight)))

    def forward(inputs, queries, *weights):

        def per_sequence(running, sequence_item):
            return (running, jax.checkpoint(one_layer)(sequence_item[0], sequence_item[1], sequence_item[2], *weights))
        running, outputs = lax.scan(per_sequence, jnp.zeros((), jnp.float32), (inputs, queries, doc_lengths))
        return outputs
    outputs, pullback = jax.vjp(forward, tokens.astype(jnp.float32), second_query.astype(jnp.float32), *float_weights)
    grads = pullback((out_grad.astype(jnp.float32), second_grad.astype(jnp.float32)))
    return (outputs[0].astype(jnp.bfloat16), grads[0].astype(jnp.bfloat16), grads[1].astype(jnp.bfloat16), grads[2], grads[3], grads[4], grads[5], grads[6], grads[7], grads[8], grads[9], grads[10])
```

```python
import functools
import math

import jax
import jax.numpy as jnp
from jax import lax
from jax.experimental import pallas as pl
from jax.experimental.pallas import tpu as pltpu
from jax.sharding import Mesh
from jax.sharding import PartitionSpec as P

HEADS = 9
KVH = 3
HD = 64
GROUP = HEADS // KVH
NEGATIVE = -1e30
EPSILON = 1e-05
ROPE_BASE = 100000.0
FACTOR = 1.0 / math.sqrt(HD)
LANES = 128
SIDE = 4
KEYS = 256
CHUNK = 256
SEQ = ("z", "x")
f32 = jnp.float32
bf16 = jnp.bfloat16

VMEM = pl.BlockSpec(memory_space=pltpu.VMEM)
SMEM = pl.BlockSpec(memory_space=pltpu.SMEM)


def params(megabytes=56):
    return pltpu.CompilerParams(vmem_limit_bytes=megabytes * 1024 * 1024)


def shape_of(dims, dtype):
    return jax.ShapeDtypeStruct(dims, dtype)


def mul(left, right):
    return lax.dot_general(left, right, (((1,), (0,)), ((), ())), preferred_element_type=f32)


def mul_nt(left, right):
    return lax.dot_general(left, right, (((1,), (1,)), ((), ())), preferred_element_type=f32)


def flip(array):
    rows, cols = array.shape
    spare = -cols % LANES
    if spare:
        array = jnp.concatenate([array, jnp.zeros((rows, spare), array.dtype)], axis=1)
    return jnp.transpose(array)[:cols]


def flip_back(array):
    rows, cols = array.shape
    spare = -rows % LANES
    if spare:
        array = jnp.concatenate([array, jnp.zeros((spare, cols), array.dtype)], axis=0)
    return jnp.transpose(array)[:, :rows]


def natural_table(table):
    return jnp.transpose(jnp.concatenate([table] * (LANES // table.shape[0]), axis=0))


def swap_halves(tile):
    lane = lax.broadcasted_iota(jnp.int32, tile.shape, 1)
    half = HD // 2
    ahead = pltpu.roll(tile, LANES - half, axis=1)
    behind = pltpu.roll(tile, half, axis=1)
    return jnp.where(lane % HD < half, ahead, behind)


def rope_kv(kv, cosine, signed_sine):
    first, second, third = kv[:, :LANES], kv[:, LANES : 2 * LANES], kv[:, 2 * LANES :]
    lane = lax.broadcasted_iota(jnp.int32, first.shape, 1)
    first = first * cosine + swap_halves(first) * signed_sine
    turned = second * cosine + swap_halves(second) * signed_sine
    return jnp.concatenate([first, jnp.where(lane < HD, turned, second), third], axis=1)


def sine_signs(sine):
    lane = lax.broadcasted_iota(jnp.int32, sine.shape, 1)
    return jnp.where(lane % HD < HD // 2, -sine, sine)


def kv_kernel(tokens, gain, weight, cos_ref, sin_ref, normed_out, kv_out):
    inputs = tokens[...].astype(f32)
    scale = lax.rsqrt(jnp.mean(inputs * inputs, axis=-1, keepdims=True) + EPSILON)
    normed = (inputs * scale * gain[...].astype(f32)).astype(bf16)
    normed_out[...] = normed
    cosine = natural_table(cos_ref[...])
    sine = sine_signs(natural_table(sin_ref[...]))
    kv_out[...] = rope_kv(mul(normed, weight[...]), cosine, sine).astype(bf16)


def query_kernel(normed, weight, cos_ref, sin_ref, second, second_grad, q1_out, q2_out, d2_out):
    flat = flip(mul(normed[...], weight[...]))
    cosine, sine = cos_ref[...], sin_ref[...]
    half = HD // 2
    parts = []
    for head in range(HEADS):
        front = flat[head * HD : head * HD + half]
        back = flat[head * HD + half : (head + 1) * HD]
        parts += [front * cosine - back * sine, back * cosine + front * sine]
    turned = (jnp.concatenate(parts, axis=0).astype(bf16) * FACTOR).astype(bf16)
    rows = second.shape[1]
    for m in range(second.shape[0]):
        q1_out[m] = turned[:, m * rows : (m + 1) * rows]
        q2_out[m] = (flip(second[m]) * FACTOR).astype(bf16)
        d2_out[m] = flip(second_grad[m])


def lane_heads(ref, group):
    return jnp.concatenate(
        [ref[(group * GROUP + h) * HD : (group * GROUP + h + 1) * HD, :] for h in range(GROUP)], axis=1
    )


def padded(block, place):
    zero = jnp.zeros_like(block)
    return jnp.concatenate([block, zero] if place % 2 == 0 else [zero, block], axis=0)


def slot_of(z, x, dz, dx, sign):
    zz = lax.rem(z + sign * dz + SIDE, SIDE)
    xx = lax.rem(x + sign * dx + SIDE, SIDE)
    return zz * SIDE + xx


def load_pieces(info, pieces, held, m):
    z, x = info[3], info[4]
    for major in range(SIDE):
        for minor in range(SIDE):
            dz, dx = (major, minor) if m == 0 else (minor, major)
            held[slot_of(z, x, dz, dx, -1)] = pieces[major][minor]


def visible_bias(info, start, first_key, rows):
    keys = first_key + lax.broadcasted_iota(jnp.int32, (KEYS, rows), 0)
    queries = info[2] * rows + lax.broadcasted_iota(jnp.int32, (KEYS, rows), 1)
    seen = (keys >= start) & (keys <= queries)
    bias = jnp.where(seen, 0.0, NEGATIVE)
    return jnp.concatenate([bias] * GROUP, axis=1)


def forward_kernel(m, info, p0, p1, p2, p3, query, start, out, flat_out, lse_out, held, acc, peak, mass):
    load_pieces(info, (p0, p1, p2, p3), held, m)
    rows = query.shape[1]
    per = KEYS // rows
    acc[...] = jnp.zeros_like(acc)
    peak[...] = jnp.full_like(peak, NEGATIVE)
    mass[...] = jnp.zeros_like(mass)

    @pl.loop(info[m], info[2] // per + 1)
    def _(step):
        block = held[pl.ds(step * per, per)].reshape(KEYS, held.shape[2])
        bias = visible_bias(info, start[...], step * KEYS, rows)
        tiles = [block[:, i * LANES : (i + 1) * LANES] for i in range(3)]
        turned = [None, jnp.transpose(tiles[1]), jnp.transpose(tiles[2])]
        for g in range(KVH):
            scores = mul(tiles[g // 2], padded(lane_heads(query, g), g)) + bias
            old = peak[g]
            top = jnp.maximum(old, jnp.max(scores, axis=0, keepdims=True))
            weights = jnp.exp(scores - top)
            decay = jnp.exp(old - top)
            place = KVH + g
            values = turned[place // 2][(place % 2) * HD : (place % 2 + 1) * HD]
            mass[g] = mass[g] * decay + jnp.sum(weights, axis=0, keepdims=True)
            acc[g] = acc[g] * decay + mul(values, weights.astype(bf16))
            peak[g] = top

    for g in range(KVH):
        lse_out[g] = peak[g] + jnp.log(mass[g])
        result = acc[g] * (1.0 / mass[g])
        for h in range(GROUP):
            head = g * GROUP + h
            flat_out[head * HD : (head + 1) * HD, :] = result[:, h * rows : (h + 1) * rows]
    out[...] = flip_back(flat_out[...].astype(bf16))


def attend_forward(m, info, pieces, query, start):
    width, rows = query.shape
    lanes = GROUP * rows
    kv_width = pieces[0].shape[-1]
    return pl.pallas_call(
        functools.partial(forward_kernel, m),
        in_specs=[SMEM] + [VMEM] * 6,
        out_specs=[VMEM] * 3,
        out_shape=[
            shape_of((rows, width), bf16),
            shape_of((width, rows), f32),
            shape_of((KVH, 1, lanes), f32),
        ],
        scratch_shapes=[
            pltpu.VMEM((SIDE * SIDE, rows, kv_width), bf16),
            pltpu.VMEM((KVH, HD, lanes), f32),
            pltpu.VMEM((KVH, 1, lanes), f32),
            pltpu.VMEM((KVH, 1, lanes), f32),
        ],
        compiler_params=params(),
        cost_estimate=pl.CostEstimate(flops=10**9, bytes_accessed=3 * 10**6, transcendentals=10**6),
        name="attention_forward",
    )(info, *pieces, query, start)


def backward_kernel(m, info, *refs):
    pieces = refs[:4]
    q_refs, d_refs, o_refs, lse_refs = refs[4:6], refs[6:8], refs[8:10], refs[10:12]
    start, cos_ref, sin_ref = refs[12:15]
    outs = refs[15:19]
    first_grad, second_grad = refs[19:21]
    held, sums, delta, dq = refs[21:]
    load_pieces(info, pieces, held, m)
    rows = q_refs[0].shape[1]
    per = KEYS // rows
    sums[...] = jnp.zeros_like(sums)
    dq[...] = jnp.zeros_like(dq)
    for a in range(2):
        for g in range(KVH):
            product = lane_heads(d_refs[a], g).astype(f32) * lane_heads(o_refs[a], g)
            delta[a, g] = jnp.sum(product, axis=0, keepdims=True)

    @pl.loop(info[m], info[2] // per + 1)
    def _(step):
        block = held[pl.ds(step * per, per)].reshape(KEYS, held.shape[2])
        bias = visible_bias(info, start[...], step * KEYS, rows)
        tiles = [block[:, i * LANES : (i + 1) * LANES] for i in range(3)]
        turned = [jnp.transpose(tiles[0]), jnp.transpose(tiles[1])]
        total = [jnp.zeros((KEYS, LANES), f32) for _ in range(3)]
        for g in range(KVH):
            place = KVH + g
            keys = turned[g // 2][(g % 2) * HD : (g % 2 + 1) * HD]
            for a in range(2):
                query = padded(lane_heads(q_refs[a], g), g)
                grad = padded(lane_heads(d_refs[a], g), place)
                scores = mul(tiles[g // 2], query) + bias
                weights = jnp.exp(scores - lse_refs[a][g])
                weight_grad = mul(tiles[place // 2], grad)
                score_grad = (weights * (weight_grad - delta[a, g])).astype(bf16)
                dq[a, g] += mul(keys, score_grad)
                total[g // 2] += mul_nt(score_grad, query)
                total[place // 2] += mul_nt(weights.astype(bf16), grad)
        joined = jnp.concatenate(total, axis=1).astype(bf16)
        sums[pl.ds(step * per, per)] = joined.reshape(per, rows, joined.shape[1])

    z, x = info[3], info[4]
    for major in range(SIDE):
        for minor in range(SIDE):
            dz, dx = (major, minor) if m == 0 else (minor, major)
            outs[major][minor] = sums[slot_of(z, x, dz, dx, 1)]
    cosine, sine = cos_ref[...], sin_ref[...]
    half = HD // 2
    first_parts, second_parts = [], []
    for g in range(KVH):
        for h in range(GROUP):
            span = slice(h * rows, (h + 1) * rows)
            own = dq[0, g][:, span] * FACTOR
            front, back = own[:half], own[half:]
            first_parts += [front * cosine + back * sine, back * cosine - front * sine]
            second_parts.append(dq[1, g][:, span] * FACTOR)
    first_grad[...] = flip_back(jnp.concatenate(first_parts, axis=0).astype(bf16))
    second_grad[...] = flip_back(jnp.concatenate(second_parts, axis=0).astype(bf16))


def attend_backward(m, info, pieces, queries, grads, outs, lses, start, cosine, sine):
    width, rows = queries[0].shape
    lanes = GROUP * rows
    kv_width = pieces[0].shape[-1]
    piece = shape_of((SIDE, rows, kv_width), bf16)
    results = pl.pallas_call(
        functools.partial(backward_kernel, m),
        in_specs=[SMEM] + [VMEM] * 15,
        out_specs=[VMEM] * 6,
        out_shape=[piece] * 4 + [shape_of((rows, width), bf16)] * 2,
        scratch_shapes=[
            pltpu.VMEM((SIDE * SIDE, rows, kv_width), bf16),
            pltpu.VMEM((SIDE * SIDE, rows, kv_width), bf16),
            pltpu.VMEM((2, KVH, 1, lanes), f32),
            pltpu.VMEM((2, KVH, HD, lanes), f32),
        ],
        compiler_params=params(),
        cost_estimate=pl.CostEstimate(flops=5 * 10**9, bytes_accessed=6 * 10**6, transcendentals=10**6),
        name="attention_backward",
    )(info, *pieces, *queries, *grads, *outs, *lses, start, cosine, sine)
    return results[:4], results[4], results[5]


def norm_back(vector, scale, gain, gradient):
    weighted = gradient * gain
    gain_grad = jnp.sum(gradient * vector * scale, axis=0, keepdims=True)
    inner = jnp.mean(weighted * vector, axis=-1, keepdims=True)
    return scale * weighted - vector * (scale * scale * scale * inner), gain_grad


def ffn_kernel(
    first, tokens, out_weight, gain, out_grad, wg, wu, wd,
    result, weight_grads, wo_grad, middle_grad, d1, gain_grad,
    middle, normed, normed_t, grad_t, result_sum, normed_grad,
):
    step = pl.program_id(0)

    @pl.when(step == 0)
    def _():
        value = tokens[...].astype(f32) + mul(first[...], out_weight[...])
        scale = lax.rsqrt(jnp.mean(value * value, axis=-1, keepdims=True) + EPSILON)
        low = (value * scale * gain[...].astype(f32)).astype(bf16)
        middle[...] = value
        normed[...] = low
        normed_t[...] = flip(low)
        grad_t[...] = flip(out_grad[...])
        result_sum[...] = value
        normed_grad[...] = jnp.zeros_like(normed_grad)

    low = normed[...]
    gate = mul(low, wg[...])
    up = mul(low, wu[...])
    sigmoid = 1.0 / (1.0 + jnp.exp(-gate))
    active = gate * sigmoid
    hidden = (active * up).astype(bf16)
    result_sum[...] += mul(hidden, wd[...])
    hidden_grad = mul_nt(out_grad[...], wd[...])
    gate_grad = (hidden_grad * up * sigmoid * (1.0 + gate * (1.0 - sigmoid))).astype(bf16)
    up_grad = (hidden_grad * active).astype(bf16)
    down = mul(grad_t[...], hidden).astype(bf16)
    gates = mul(normed_t[...], gate_grad).astype(bf16)
    ups = mul(normed_t[...], up_grad).astype(bf16)
    for i in range(CHUNK // LANES):
        span = slice(i * LANES, (i + 1) * LANES)
        weight_grads[i, 0] = gates[:, span]
        weight_grads[i, 1] = ups[:, span]
        weight_grads[i, 2] = down[:, span]
    normed_grad[...] += mul_nt(gate_grad, wg[...]) + mul_nt(up_grad, wu[...])

    @pl.when(step == pl.num_programs(0) - 1)
    def _():
        result[...] = result_sum[...].astype(bf16)
        value = middle[...]
        scale = lax.rsqrt(jnp.mean(value * value, axis=-1, keepdims=True) + EPSILON)
        part, gains = norm_back(value, scale, gain[...].astype(f32), normed_grad[...])
        gain_grad[...] = gains
        total = out_grad[...].astype(f32) + part
        middle_grad[...] = total
        branch = total.astype(bf16)
        wo_grad[...] = mul(flip(first[...]), branch).astype(bf16)
        flat = flip(mul_nt(branch, out_weight[...]).astype(bf16))
        rows = d1.shape[2]
        for m in range(d1.shape[0]):
            d1[m] = flat[:, m * rows : (m + 1) * rows]


def feed_forward(first, tokens, out_weight, gain, out_grad, wg, wu, wd, micro):
    rows, width = tokens.shape
    hidden = wg.shape[1]
    steps = hidden // CHUNK
    per = CHUNK // LANES

    def whole(*dims):
        return pl.BlockSpec(dims, lambda i: (0,) * len(dims))

    return pl.pallas_call(
        ffn_kernel,
        grid=(steps,),
        in_specs=[
            whole(rows, width),
            whole(rows, width),
            whole(width, width),
            whole(1, width),
            whole(rows, width),
            pl.BlockSpec((width, CHUNK), lambda i: (0, i)),
            pl.BlockSpec((width, CHUNK), lambda i: (0, i)),
            pl.BlockSpec((CHUNK, width), lambda i: (i, 0)),
        ],
        out_specs=[
            whole(rows, width),
            pl.BlockSpec((per, 3, width, LANES), lambda i: (i, 0, 0, 0)),
            whole(width, width),
            whole(rows, width),
            whole(micro, width, rows // micro),
            whole(1, width),
        ],
        out_shape=[
            shape_of((rows, width), bf16),
            shape_of((hidden // LANES, 3, width, LANES), bf16),
            shape_of((width, width), bf16),
            shape_of((rows, width), f32),
            shape_of((micro, width, rows // micro), bf16),
            shape_of((1, width), f32),
        ],
        scratch_shapes=[
            pltpu.VMEM((rows, width), f32),
            pltpu.VMEM((rows, width), bf16),
            pltpu.VMEM((width, rows), bf16),
            pltpu.VMEM((width, rows), bf16),
            pltpu.VMEM((rows, width), f32),
            pltpu.VMEM((rows, width), f32),
        ],
        compiler_params=params(),
        cost_estimate=pl.CostEstimate(flops=6 * 10**9, bytes_accessed=14 * 10**6, transcendentals=10**6),
        name="feed_forward",
    )(first, tokens, out_weight, gain, out_grad, wg, wu, wd)


def query_back_kernel(normed, grad, weight, weight_grad, normed_grad):
    weight_grad[...] = mul(flip(normed[...]), grad[...]).astype(bf16)
    normed_grad[...] = mul_nt(grad[...], weight[...])


def input_back_kernel(
    normed, kv_grad, weight, cos_ref, sin_ref, partial, tokens, gain, middle_grad,
    weight_grad, input_grad, gain_grad,
):
    cosine = natural_table(cos_ref[...])
    sine = sine_signs(natural_table(sin_ref[...]))
    low = rope_kv(kv_grad[...], cosine, -sine).astype(bf16)
    weight_grad[...] = mul(flip(normed[...]), low).astype(bf16)
    normed_grad = partial[...] + mul_nt(low, weight[...])
    inputs = tokens[...].astype(f32)
    scale = lax.rsqrt(jnp.mean(inputs * inputs, axis=-1, keepdims=True) + EPSILON)
    part, gains = norm_back(inputs, scale, gain[...].astype(f32), normed_grad)
    gain_grad[...] = gains
    input_grad[...] = (middle_grad[...] + part).astype(bf16)


def simple(kernel, outs, args, name, flops):
    return pl.pallas_call(
        kernel,
        in_specs=[VMEM] * len(args),
        out_specs=[VMEM] * len(outs),
        out_shape=outs,
        compiler_params=params(),
        cost_estimate=pl.CostEstimate(flops=flops, bytes_accessed=2 * 10**6, transcendentals=0),
        name=name,
    )(*args)


def shift(value, axis, distance):
    size = lax.axis_size(axis)
    return lax.ppermute(value, axis, [(i, (i + distance) % size) for i in range(size)])


def collect(value, axis):
    return [value] + [shift(value, axis, k) for k in range(1, SIDE)]


def gather_pieces(value, first, second):
    return collect(jnp.stack(collect(value, first)), second)


def scatter_pieces(pieces, first, second):
    def exchange(parts, axis):
        total = parts[0].astype(f32)
        for k in range(1, SIDE):
            total = total + shift(parts[k], axis, k).astype(f32)
        return total

    held = exchange(pieces, first).astype(bf16)
    return exchange([held[k] for k in range(SIDE)], second)


def reduce_all(value):
    rows, lanes = value.shape
    core = lax.axis_index("core")
    halves = value.reshape(2, rows // 2, lanes)
    mine = lax.dynamic_index_in_dim(halves, core, 0, False)
    other = lax.dynamic_index_in_dim(halves, 1 - core, 0, False)
    held = (mine.astype(f32) + shift(other, "core", 1).astype(f32)).astype(bf16)
    places = SIDE * SIDE
    parts = lax.all_to_all(held.reshape(places, rows // (2 * places), lanes), SEQ, 0, 0)
    held = jnp.sum(parts.astype(f32), axis=0).astype(bf16)
    total = held.astype(f32)
    for k in range(1, SIDE):
        total = total + shift(held, "y", k).astype(f32)
    held = total.astype(bf16)
    spread = jnp.broadcast_to(held[None], (places,) + held.shape)
    held = lax.all_to_all(spread, SEQ, 0, 0).reshape(rows // 2, lanes)
    other = shift(held, "core", 1)
    first = jnp.where(core == 0, held, other)
    second = jnp.where(core == 0, other, held)
    return jnp.concatenate([first, second], axis=0)


def lane_tiles(array):
    rows, cols = array.shape
    spare = -cols % LANES
    array = jnp.pad(array, ((0, 0), (0, spare)))
    return array.reshape(rows, -1, LANES).transpose(1, 0, 2).reshape(-1, LANES)


def from_tiles(tiles, rows, cols):
    tiles = tiles.reshape(-1, rows, LANES).transpose(1, 0, 2).reshape(rows, -1)
    return tiles[:, :cols].astype(f32)


def per_device(
    tokens,
    doc_lengths,
    second_query,
    second_grad,
    out_grad,
    first_gain,
    query_weight,
    key_weight,
    value_weight,
    output_weight,
    second_gain,
    gate_weight,
    up_weight,
    down_weight,
):
    micro, rows, width = tokens.shape
    kwidth = key_weight.shape[1]
    hidden = gate_weight.shape[1]
    z, x = lax.axis_index("z"), lax.axis_index("x")
    own = z * SIDE + x
    entries = doc_lengths.shape[1]
    upto = lax.iota(jnp.int32, entries)
    ends = jnp.sum(
        doc_lengths[:, None, :] * (upto[None, :] <= upto[:, None]).astype(jnp.int32)[None], axis=2
    )
    places = own * rows + lax.iota(jnp.int32, rows)
    passed = (ends[:, :, None] <= places[None, None, :]).astype(jnp.int32)
    starts = jnp.sum(passed * doc_lengths[:, :, None], axis=1)
    position = (places[None] - starts).reshape(1, micro * rows)
    frequency = ROPE_BASE ** (-(lax.iota(f32, HD // 2) * 2.0) / HD)
    angles = position.astype(f32) * frequency[:, None]
    cosine, sine = jnp.cos(angles), jnp.sin(angles)
    info = jnp.concatenate([starts[:, 0] // KEYS, jnp.stack([own, z, x])])

    flat_tokens = tokens.reshape(micro * rows, width)
    gain_one, gain_two = first_gain.reshape(1, width), second_gain.reshape(1, width)
    kv_weight = jnp.concatenate([key_weight, value_weight], axis=1)
    total = micro * rows
    normed, kv = simple(
        kv_kernel,
        [shape_of((total, width), bf16), shape_of((total, 2 * kwidth), bf16)],
        (flat_tokens, gain_one, kv_weight, cosine, sine),
        "key_value",
        2 * 10**8,
    )
    kv = kv.reshape(micro, rows, 2 * kwidth)
    axes = [("x", "z"), ("z", "x")]
    pieces = [gather_pieces(kv[m], *axes[m]) for m in range(micro)]
    turned = shape_of((micro, width, rows), bf16)
    q1, q2, d2 = simple(
        query_kernel,
        [turned] * 3,
        (normed, query_weight, cosine, sine, second_query, second_grad),
        "query",
        2 * 10**8,
    )
    first = [
        attend_forward(m, info, pieces[m], q1[m], starts[m : m + 1]) for m in range(micro)
    ]
    first_low = jnp.concatenate([f[0] for f in first], axis=0)
    result, main_grads, wo_grad, middle_grad, d1, gain_two_grad = feed_forward(
        first_low,
        flat_tokens,
        output_weight,
        gain_two,
        out_grad.reshape(total, width),
        gate_weight,
        up_weight,
        down_weight,
        micro,
    )
    main = reduce_all(main_grads.reshape(-1, LANES)).reshape(main_grads.shape)
    query_grads, second_grads, kv_grads = [], [], []
    for m in range(micro):
        second = attend_forward(m, info, pieces[m], q2[m], starts[m : m + 1])
        span = slice(m * rows, (m + 1) * rows)
        sums, first_part, second_part = attend_backward(
            m,
            info,
            pieces[m],
            (q1[m], q2[m]),
            (d1[m], d2[m]),
            (first[m][1], second[1]),
            (first[m][2], second[2]),
            starts[m : m + 1],
            cosine[:, span],
            sine[:, span],
        )
        query_grads.append(first_part)
        second_grads.append(second_part)
        kv_grads.append(scatter_pieces(sums, *axes[m][::-1]))
    query_grad = jnp.concatenate(query_grads, axis=0)
    wq_grad, normed_part = simple(
        query_back_kernel,
        [shape_of((width, width), bf16), shape_of((total, width), f32)],
        (normed, query_grad, query_weight),
        "query_back",
        3 * 10**8,
    )
    wkv_grad, input_grad, gain_one_grad = simple(
        input_back_kernel,
        [
            shape_of((width, 2 * kwidth), bf16),
            shape_of((total, width), bf16),
            shape_of((1, width), f32),
        ],
        (
            normed,
            jnp.concatenate(kv_grads, axis=0),
            kv_weight,
            cosine,
            sine,
            normed_part,
            flat_tokens,
            gain_one,
            middle_grad,
        ),
        "input_back",
        2 * 10**8,
    )
    gains = lane_tiles(jnp.concatenate([gain_one_grad, gain_two_grad], axis=0).astype(bf16))
    parts = [lane_tiles(wo_grad), lane_tiles(wq_grad), lane_tiles(wkv_grad), gains]
    used = sum(part.shape[0] for part in parts)
    spare = -used % (64 * 8)
    tail = reduce_all(jnp.concatenate(parts + [jnp.zeros((spare, LANES), bf16)], axis=0))
    tiles = -(-width // LANES)
    first_end = tiles * width
    second_end = 2 * first_end
    third_end = second_end + 2 * kwidth // LANES * width
    kv_total = from_tiles(tail[second_end:third_end], width, 2 * kwidth)
    gain_total = from_tiles(tail[third_end : third_end + 2 * tiles], 2, width)
    return (
        result.reshape(micro, rows, width),
        input_grad.reshape(micro, rows, width),
        jnp.stack(second_grads),
        gain_total[0],
        from_tiles(tail[first_end:second_end], width, width),
        kv_total[:, :kwidth],
        kv_total[:, kwidth:],
        from_tiles(tail[:first_end], width, width),
        gain_total[1],
        from_tiles(main[:, 0], width, hidden),
        from_tiles(main[:, 1], width, hidden),
        from_tiles(main[:, 2], width, hidden).T,
    )


def solution(mesh):
    grid = Mesh(mesh.devices.reshape(SIDE, SIDE, SIDE, 2), ("z", "x", "y", "core"))
    split = P(("y", "core"), SEQ, None)
    in_specs = (split, P(("y", "core"), None), split, split, split) + (P(),) * 9
    out_specs = (split, split, split) + (P(),) * 9
    return jax.shard_map(
        per_device, mesh=grid, in_specs=in_specs, out_specs=out_specs, check_vma=False
    )
```

```python
import functools
import math

import jax
import jax.numpy as jnp
from jax import lax
from jax.experimental import pallas as pl
from jax.experimental.pallas import tpu as pltpu
from jax.sharding import Mesh
from jax.sharding import PartitionSpec as P

HEADS = 9
KVH = 3
HD = 64
HALF = HD // 2
GROUP = HEADS // KVH
NEGATIVE = -1e30
EPSILON = 1e-05
ROPE_BASE = 100000.0
FACTOR = 1.0 / math.sqrt(HD)
LANES = 128
SIDE = 4
KEYS = 256
CHUNK = 384
SEQ = ("z", "x")
SIMPLE = {"kv_weights": 2.0, "input_back": 1.0, "prepare": 1.0, "query": 1.0}
f32 = jnp.float32
bf16 = jnp.bfloat16

VMEM = pl.BlockSpec(memory_space=pltpu.VMEM)
SMEM = pl.BlockSpec(memory_space=pltpu.SMEM)


def cost(microseconds):
    return pl.CostEstimate(flops=int(microseconds * 10**9), bytes_accessed=1000, transcendentals=0)


ANY = pl.BlockSpec(memory_space=pl.ANY)


def params(megabytes=56):
    return pltpu.CompilerParams(vmem_limit_bytes=megabytes * 1024 * 1024)


def shape_of(dims, dtype):
    return jax.ShapeDtypeStruct(dims, dtype)


def mul(left, right):
    return lax.dot_general(left, right, (((1,), (0,)), ((), ())), preferred_element_type=f32)


def mul_nt(left, right):
    return lax.dot_general(left, right, (((1,), (1,)), ((), ())), preferred_element_type=f32)


def flip(array):
    rows, cols = array.shape
    spare = -cols % LANES
    if spare:
        array = jnp.concatenate([array, jnp.zeros((rows, spare), array.dtype)], axis=1)
    extra = -rows % LANES
    if extra:
        array = jnp.concatenate([array, jnp.zeros((extra, cols + spare), array.dtype)], axis=0)
    return jnp.transpose(array)[:cols, :rows]


def side_by_side(ref):
    return jnp.concatenate([ref[m] for m in range(ref.shape[0])], axis=1)


def own_block():
    return lax.axis_index("z") * SIDE + lax.axis_index("x")


def far_block():
    return SIDE * SIDE - 1 - own_block()


def turn(flat, cosine, sine, heads):
    parts = []
    for head in range(heads):
        front = flat[head * HD : head * HD + HALF]
        back = flat[head * HD + HALF : (head + 1) * HD]
        parts += [front * cosine - back * sine, back * cosine + front * sine]
    return parts


def simple(kernel, in_specs, outs, args, name):
    return pl.pallas_call(
        kernel,
        in_specs=in_specs,
        out_specs=[VMEM] * len(outs),
        out_shape=outs,
        compiler_params=params(),
        cost_estimate=cost(SIMPLE[name]),
        name=name,
    )(*args)


def prepare_kernel(lengths, tokens, gain, wk, wv, normed_out, kv_out, cos_out, sin_out, starts, far_starts):
    micro, _, rows = tokens.shape
    lane = lax.broadcasted_iota(jnp.int32, (1, rows), 1)
    places = own_block() * rows + lane
    far_places = far_block() * rows + lane
    positions = []
    for m in range(micro):
        start = jnp.zeros((1, rows), jnp.int32)
        far = jnp.zeros((1, rows), jnp.int32)
        end = jnp.int32(0)
        for j in range(lengths.shape[1]):
            length = lengths[m, j]
            end = end + length
            start = start + jnp.where(places >= end, length, 0)
            far = far + jnp.where(far_places >= end, length, 0)
        starts[m] = start
        far_starts[m] = far
        positions.append(places - start)
    order = lax.broadcasted_iota(jnp.int32, (HALF, micro * rows), 0).astype(f32)
    frequency = jnp.exp(order * (-2.0 * math.log(ROPE_BASE) / HD))
    angles = jnp.concatenate(positions, axis=1).astype(f32) * frequency
    cosine, sine = jnp.cos(angles), jnp.sin(angles)
    cos_out[...] = cosine
    sin_out[...] = sine
    inputs = side_by_side(tokens).astype(f32)
    scale = lax.rsqrt(jnp.mean(inputs * inputs, axis=0, keepdims=True) + EPSILON)
    normed = (inputs * scale * gain[...].astype(f32)).astype(bf16)
    width = tokens.shape[1]
    for m in range(micro):
        span = slice(m * rows, (m + 1) * rows)
        normed_out[m, :width] = normed[:, span]
        base = width
        for table in (cosine, sine):
            high = table[:, span].astype(bf16)
            normed_out[m, base : base + HALF] = high
            normed_out[m, base + HALF : base + 2 * HALF] = (table[:, span] - high.astype(f32)).astype(bf16)
            base += 2 * HALF
    parts = turn(mul(wk[...], normed), cosine, sine, KVH)
    flat = jnp.concatenate(parts + [mul(wv[...], normed)], axis=0).astype(bf16)
    for m in range(micro):
        kv_out[m] = flip(flat[:, m * rows : (m + 1) * rows])


def query_kernel(normed, weight, cos_ref, sin_ref, q1_out):
    width = weight.shape[0]
    flat = mul(flip(weight[...]), jnp.concatenate([normed[m, :width] for m in range(normed.shape[0])], axis=1))
    parts = turn(flat, cos_ref[...], sin_ref[...], HEADS)
    turned = (jnp.concatenate(parts, axis=0).astype(bf16) * FACTOR).astype(bf16)
    rows = q1_out.shape[2]
    for m in range(q1_out.shape[0]):
        q1_out[m] = turned[:, m * rows : (m + 1) * rows]


def lane_heads(ref, group):
    return jnp.concatenate(
        [ref[(group * GROUP + h) * HD : (group * GROUP + h + 1) * HD, :] for h in range(GROUP)], axis=1
    )


def padded(block, place):
    zero = jnp.zeros_like(block)
    return jnp.concatenate([block, zero] if place % 2 == 0 else [zero, block], axis=0)


def visible_bias(start, block, first_key, rows):
    keys = first_key + lax.broadcasted_iota(jnp.int32, (KEYS, rows), 0)
    queries = block * rows + lax.broadcasted_iota(jnp.int32, (KEYS, rows), 1)
    seen = (keys >= start) & (keys <= queries)
    bias = jnp.where(seen, 0.0, NEGATIVE)
    return jnp.concatenate([bias] * GROUP, axis=1)


def key_steps(start, block, rows):
    per = KEYS // rows
    return jnp.min(start) // KEYS, block // per + 1


def forward_kernel(far, held, query_ref, starts, low_out, flat_out, lse_out, acc, peak, mass, query):
    block_place = far_block() if far else own_block()
    scale = FACTOR if far else 1.0
    query[...] = (query_ref[0] * scale).astype(bf16)
    rows = query.shape[1]
    per = KEYS // rows
    acc[...] = jnp.zeros_like(acc)
    peak[...] = jnp.full_like(peak, NEGATIVE)
    mass[...] = jnp.zeros_like(mass)
    start = starts[0]
    first_step, last_step = key_steps(start, block_place, rows)

    @pl.loop(first_step, last_step)
    def _(step):
        block = held[pl.ds(step * per, per), 0].reshape(KEYS, held.shape[3])
        bias = visible_bias(start, block_place, step * KEYS, rows)
        tiles = [block[:, i * LANES : (i + 1) * LANES] for i in range(3)]
        turned = [None, jnp.transpose(tiles[1]), jnp.transpose(tiles[2])]
        for g in range(KVH):
            scores = mul(tiles[g // 2], padded(lane_heads(query, g), g)) + bias
            old = peak[g]
            top = jnp.maximum(old, jnp.max(scores, axis=0, keepdims=True))
            weights = jnp.exp(scores - top)
            decay = jnp.exp(old - top)
            place = KVH + g
            values = turned[place // 2][(place % 2) * HD : (place % 2 + 1) * HD]
            mass[g] = mass[g] * decay + jnp.sum(weights, axis=0, keepdims=True)
            acc[g] = acc[g] * decay + mul(values, weights.astype(bf16))
            peak[g] = top

    for g in range(KVH):
        lse_out[0, g] = peak[g] + jnp.log(mass[g])
        result = acc[g] * (1.0 / mass[g])
        for h in range(GROUP):
            head = g * GROUP + h
            flat_out[0, head * HD : (head + 1) * HD, :] = result[:, h * rows : (h + 1) * rows]
    low_out[...] = flat_out[...].astype(bf16)


def one_of(dims, axis=0):
    block = tuple(1 if i == axis else n for i, n in enumerate(dims))
    return pl.BlockSpec(block, lambda m: tuple(m if i == axis else 0 for i in range(len(dims))))


def attend_forward(far, kv, query, starts):
    micro, width, rows = query.shape
    lanes = GROUP * rows
    low = shape_of(query.shape, bf16)
    flat = shape_of(query.shape, f32)
    lse = shape_of((micro, KVH, 1, lanes), f32)
    return pl.pallas_call(
        functools.partial(forward_kernel, far),
        grid=(micro,),
        in_specs=[one_of(kv.shape, 1), one_of(query.shape), one_of(starts.shape)],
        out_specs=[one_of(v.shape) for v in (low, flat, lse)],
        out_shape=[low, flat, lse],
        scratch_shapes=[
            pltpu.VMEM((KVH, HD, lanes), f32),
            pltpu.VMEM((KVH, 1, lanes), f32),
            pltpu.VMEM((KVH, 1, lanes), f32),
            pltpu.VMEM((width, rows), bf16),
        ],
        compiler_params=params(),
        cost_estimate=cost(2.5),
        name="attention_forward",
    )(kv, query, starts)


def backward_kernel(
    held, q1_ref, q2_ref, d1_ref, d2_ref, o1, o2, lse1, lse2, starts, far_starts, cos_ref, sin_ref,
    kv_out, first_grad, second_grad, sums, delta, dq, query2,
):
    rows = q1_ref.shape[2]
    per = KEYS // rows
    query2[...] = (q2_ref[0] * FACTOR).astype(bf16)
    sums[...] = jnp.zeros_like(sums)
    dq[...] = jnp.zeros_like(dq)

    def attention(a, q_ref, d_ref, o_ref, lse_ref, start, block_place):
        for g in range(KVH):
            product = lane_heads(d_ref, g).astype(f32) * lane_heads(o_ref, g)
            delta[a, g] = jnp.sum(product, axis=0, keepdims=True)
        first_step, last_step = key_steps(start, block_place, rows)

        @pl.loop(first_step, last_step)
        def _(step):
            block = held[pl.ds(step * per, per), 0].reshape(KEYS, held.shape[3])
            bias = visible_bias(start, block_place, step * KEYS, rows)
            tiles = [block[:, i * LANES : (i + 1) * LANES] for i in range(3)]
            turned = [jnp.transpose(tiles[0]), jnp.transpose(tiles[1])]
            total = [None] * 3

            def add(place, value):
                total[place] = value if total[place] is None else total[place] + value

            for g in range(KVH):
                place = KVH + g
                keys = turned[g // 2][(g % 2) * HD : (g % 2 + 1) * HD]
                query = padded(lane_heads(q_ref, g), g)
                grad = padded(lane_heads(d_ref, g), place)
                scores = mul(tiles[g // 2], query) + bias
                weights = jnp.exp(scores - lse_ref[0, g])
                weight_grad = mul(tiles[place // 2], grad)
                score_grad = (weights * (weight_grad - delta[a, g])).astype(bf16)
                dq[a, g] += mul(keys, score_grad)
                add(g // 2, mul_nt(score_grad, query))
                add(place // 2, mul_nt(weights.astype(bf16), grad))
            joined = jnp.concatenate(total, axis=1)
            sums[pl.ds(step * per, per)] += joined.reshape(per, rows, joined.shape[1])

    attention(0, q1_ref.at[0], d1_ref.at[0], o1.at[0], lse1, starts[0], own_block())
    attention(1, query2, d2_ref.at[0], o2.at[0], lse2, far_starts[0], far_block())
    kv_out[:, 0] = sums[...].astype(bf16)
    cosine, sine = cos_ref[...], -sin_ref[...]
    for g in range(KVH):
        for h in range(GROUP):
            head = g * GROUP + h
            lanes = slice(h * rows, (h + 1) * rows)
            target = slice(head * HD, (head + 1) * HD)
            parts = turn(dq[0, g][:, lanes] * FACTOR, cosine, sine, 1)
            first_grad[0, target, :] = jnp.concatenate(parts, axis=0).astype(bf16)
            second_grad[0, target, :] = (dq[1, g][:, lanes] * FACTOR).astype(bf16)


def attend_backward(kv, *arrays):
    micro, width, rows = arrays[0].shape
    lanes = GROUP * rows
    blocks, _, _, kv_width = kv.shape
    part = shape_of((micro, width, rows), bf16)
    table = pl.BlockSpec((HALF, rows), lambda m: (0, m))
    return pl.pallas_call(
        backward_kernel,
        grid=(micro,),
        in_specs=[one_of(kv.shape, 1)] + [one_of(v.shape) for v in arrays[:-2]] + [table] * 2,
        out_specs=[one_of(kv.shape, 1)] + [one_of(part.shape)] * 2,
        out_shape=[shape_of(kv.shape, bf16), part, part],
        scratch_shapes=[
            pltpu.VMEM((blocks, rows, kv_width), f32),
            pltpu.VMEM((2, KVH, 1, lanes), f32),
            pltpu.VMEM((2, KVH, HD, lanes), f32),
            pltpu.VMEM((width, rows), bf16),
        ],
        compiler_params=params(),
        cost_estimate=cost(7),
        name="attention_backward",
    )(kv, *arrays)


def kv_weights_kernel(sums, normed, starts, far_starts, k_out, v_out):
    micro, _, rows = starts.shape
    width = v_out.shape[0]
    cut = KVH * HD
    per = KEYS // rows
    k_out[...] = jnp.zeros_like(k_out)
    v_out[...] = jnp.zeros_like(v_out)
    for m in range(micro):

        def add(step):
            block = sums[pl.ds(step * per, per), m].reshape(KEYS, sums.shape[3])
            inner = [normed[step * per + i, m] for i in range(per)]
            values = jnp.concatenate([v[:width] for v in inner], axis=1)
            tables = jnp.concatenate([v[width:] for v in inner], axis=1).astype(f32)
            cosine = tables[:HALF] + tables[HALF : 2 * HALF]
            sine = tables[2 * HALF : 3 * HALF] + tables[3 * HALF :]
            flat = jnp.concatenate(
                [jnp.transpose(block[:, :LANES]), jnp.transpose(block[:, LANES : 2 * LANES])[: cut - LANES]], axis=0
            )
            keys = jnp.concatenate(turn(flat.astype(f32), cosine, -sine, KVH), axis=0).astype(bf16)
            k_out[...] += mul_nt(keys, values)
            v_out[...] += mul(values, block[:, LANES:])

        near = key_steps(starts[m], own_block(), rows)
        far = key_steps(far_starts[m], far_block(), rows)
        pl.loop(*near)(add)

        @pl.loop(*far)
        def _(step):
            pl.when((step < near[0]) | (step >= near[1]))(lambda: add(step))


def norm_back(vector, scale, gain, gradient):
    weighted = gradient * gain
    gain_grad = jnp.sum(gradient * vector * scale, axis=1, keepdims=True)
    inner = jnp.mean(weighted * vector, axis=0, keepdims=True)
    return scale * weighted - vector * (scale * scale * scale * inner), gain_grad


def ffn_kernel(
    last, core, first, tokens, out_weight, gain, out_grad, wg, wu, wd, *refs,
):
    step = pl.program_id(0)
    micro, width, rows = tokens.shape
    if last:
        before, result_before, grad_before, received = refs[:4]
        result, main0, main1, middle_grad, d1, gain_grad, wo_grad = refs[4:11]
        normed, normed_t, grad, grad_t, result_sum, normed_grad = refs[11:]
        middle = before
    else:
        main, middle, result_sum, normed_grad = refs[:4]
        normed, normed_t, grad, grad_t = refs[4:]

    @pl.when(step == 0)
    def _():
        if last:
            value = before[...]
            result_sum[...] = result_before[...]
            normed_grad[...] = grad_before[...]
        else:
            value = side_by_side(tokens).astype(f32) + mul(flip(out_weight[...]), side_by_side(first))
            middle[...] = value
            result_sum[...] = jnp.zeros_like(result_sum)
            normed_grad[...] = jnp.zeros_like(normed_grad)
        scale = lax.rsqrt(jnp.mean(value * value, axis=0, keepdims=True) + EPSILON)
        low = (value * scale * gain[...].astype(f32)).astype(bf16)
        normed_t[...] = low
        normed[...] = flip(low)
        flat = side_by_side(out_grad)
        grad_t[...] = flat
        grad[...] = flip(flat)

    low = normed[...]
    gate = mul(low, wg[...])
    up = mul(low, wu[...])
    sigmoid = 1.0 / (1.0 + jnp.exp(-gate))
    active = gate * sigmoid
    hidden = (active * up).astype(bf16)
    result_sum[...] += mul_nt(hidden, wd[...])
    hidden_grad = mul(grad[...], wd[...])
    gate_grad = (hidden_grad * up * sigmoid * (1.0 + gate * (1.0 - sigmoid))).astype(bf16)
    up_grad = (hidden_grad * active).astype(bf16)
    parts = (mul(normed_t[...], gate_grad), mul(normed_t[...], up_grad), mul(grad_t[...], hidden))
    for i in range(CHUNK // LANES):
        span = slice(i * LANES, (i + 1) * LANES)
        for k, part in enumerate(parts):
            rows_at = slice((i * 3 + k) * width, (i * 3 + k + 1) * width)
            value = part[:, span].astype(bf16)
            if last:
                value = (value.astype(f32) + received[rows_at].astype(f32)).astype(bf16)
                for index, target in enumerate((main0, main1)):
                    pl.when(step == index)(functools.partial(target.__setitem__, rows_at, value))
            else:
                main[rows_at] = value
    normed_grad[...] += mul_nt(gate_grad, wg[...]) + mul_nt(up_grad, wu[...])
    if not last:
        return

    @pl.when(step == pl.num_programs(0) - 1)
    def _():
        value = middle[...]
        final = (value + flip(result_sum[...])).astype(bf16)
        scale = lax.rsqrt(jnp.mean(value * value, axis=0, keepdims=True) + EPSILON)
        part, gains = norm_back(value, scale, gain[...].astype(f32), flip(normed_grad[...]))
        gain_grad[...] = gains
        total = grad_t[...].astype(f32) + part
        middle_grad[...] = total
        branch = total.astype(bf16)
        wo_grad[...] = mul_nt(side_by_side(first), branch).astype(bf16)
        back = mul(out_weight[...], branch).astype(bf16)
        for m in range(micro):
            span = slice(m * rows, (m + 1) * rows)
            d1[m] = back[:, span]
            result[m] = final[:, span]


def pack_rows(target, base, array):
    rows, cols = array.shape
    for i in range(-(-cols // LANES)):
        span = array[:, i * LANES : (i + 1) * LANES]
        if span.shape[1] < LANES:
            span = jnp.concatenate([span, jnp.zeros((rows, LANES - span.shape[1]), span.dtype)], axis=1)
        target[base : base + rows] = span
        base += rows
    return base


def main_rows(width):
    used = CHUNK // LANES * 3 * width
    unit = SIDE * SIDE * SIDE * 8
    return -(-used // unit) * unit


def feed_forward(core, first, tokens, out_weight, gain, out_grad, wg, wu, wd, before):
    micro, width, rows = tokens.shape
    total = micro * rows
    hidden = wg.shape[1]
    steps = hidden // 2 // CHUNK
    block = pl.BlockSpec((CHUNK // LANES * 3 * width, LANES), lambda i, c: (i, 0))
    first_block = pl.BlockSpec((CHUNK // LANES * 3 * width, LANES), lambda i, c: (0, 0))
    last = len(before) > 0

    def whole(*dims):
        return pl.BlockSpec(dims, lambda i, c: (0,) * len(dims))

    def column(i, c):
        side = c[0] if last else 1 - c[0]
        return (0, side * steps + i)

    weight = pl.BlockSpec((width, CHUNK), column)
    flat, natural = shape_of((width, total), f32), shape_of((total, width), f32)
    spec, tall = whole(width, total), whole(total, width)
    token_spec, token_shape = whole(micro, width, rows), shape_of((micro, width, rows), bf16)
    if last:
        outs = [
            (token_shape, token_spec),
            (shape_of((main_rows(width), LANES), bf16), first_block),
            (shape_of((main_rows(width), LANES), bf16), first_block),
            (flat, spec),
            (token_shape, token_spec),
            (shape_of((width, 1), f32), whole(width, 1)),
            (shape_of((width, width), bf16), whole(width, width)),
        ]
        more = [spec, tall, tall, block]
        scratch = [pltpu.VMEM((total, width), f32)] * 2
    else:
        outs = [
            (shape_of((hidden // 2 // LANES * 3 * width, LANES), bf16), block),
            (flat, spec),
            (natural, tall),
            (natural, tall),
        ]
        more, scratch = [], []
    low = [pltpu.VMEM((total, width), bf16), pltpu.VMEM((width, total), bf16)]
    return pl.pallas_call(
        functools.partial(ffn_kernel, last),
        grid_spec=pltpu.PrefetchScalarGridSpec(
            num_scalar_prefetch=1,
            grid=(steps,),
            in_specs=[
                token_spec,
                token_spec,
                whole(width, width),
                whole(width, 1),
                token_spec,
                weight,
                weight,
                weight,
            ]
            + more,
            out_specs=[v[1] for v in outs],
            scratch_shapes=low * 2 + scratch,
        ),
        out_shape=[v[0] for v in outs],
        compiler_params=params(),
        cost_estimate=cost(3),
        name="feed_forward",
    )(core, first, tokens, out_weight, gain, out_grad, wg, wu, wd, *before)


def query_back_kernel(
    normed, grad_ref, weight, wk_grad, wv_grad, wo_grad, gain_two_grad, normed_grad, kept, away, packed
):
    grad = side_by_side(grad_ref)
    width = weight.shape[0]
    values = jnp.concatenate([normed[m, :width] for m in range(normed.shape[0])], axis=1)
    normed_grad[...] = mul(weight[...], grad)
    lane = lax.broadcasted_iota(jnp.int32, (width, LANES), 1)
    gains = flip(jnp.where(lane == 0, gain_two_grad[...], 0.0))[:16]
    base = 0
    for array in (mul_nt(values, grad), wk_grad[...], wv_grad[...], wo_grad[...], gains):
        base = pack_rows(packed, base, array.astype(bf16))
    packed[base:] = jnp.zeros((packed.shape[0] - base, LANES), bf16)
    unit = kept.shape[1]
    for dy in range(SIDE):
        for target, dc in ((kept, 0), (away, 1)):
            target[dy] = packed[pl.ds(pl.multiple_of(place_of(dc, dy, 1) * unit, 16), unit)]


def tail_rows(width):
    tiles = -(-width // LANES)
    used = tiles * (2 * width + KVH * HD + 16) + (2 * KVH * HD // LANES - 1) * width
    unit = 2 * SIDE * SIDE * SIDE * 8
    return -(-used // unit) * (unit // 2)


def place_of(dc, dy, sign):
    cc = lax.rem(lax.axis_index("core") + dc, 2)
    yy = lax.rem(lax.axis_index("y") + sign * dy + SIDE, SIDE)
    return cc * SIDE + yy


def input_back_kernel(
    kv_grad, wk, wv, cos_ref, sin_ref, partial, tokens, gain, middle_grad, second, input_grad, second_grad
):
    second_grad[...] = second[...]
    micro, width, rows = tokens.shape
    flat = jnp.concatenate(
        [flip(kv_grad[m * rows : (m + 1) * rows].astype(f32)) for m in range(micro)], axis=1
    )
    cut = KVH * HD
    parts = turn(flat[:cut], cos_ref[...], -sin_ref[...], KVH)
    low = jnp.concatenate(parts + [flat[cut:]], axis=0).astype(bf16)
    weights = flip(jnp.concatenate([wk[...], wv[...]], axis=0))
    normed_grad = partial[...] + mul(weights, low)
    inputs = side_by_side(tokens).astype(f32)
    scale = lax.rsqrt(jnp.mean(inputs * inputs, axis=0, keepdims=True) + EPSILON)
    part, _ = norm_back(inputs, scale, gain[...].astype(f32), normed_grad)
    final = (middle_grad[...] + part).astype(bf16)
    for m in range(micro):
        input_grad[m] = final[:, m * rows : (m + 1) * rows]


def unpack_tail_kernel(kept, away, wq, wk, wv, gain, q_out, k_out, v_out, o_out, gain_one, gain_two, held):
    unit = kept.shape[1]
    for dy in range(SIDE):
        for source, dc in ((kept, 0), (away, 1)):
            held[pl.ds(pl.multiple_of(place_of(dc, dy, -1) * unit, 16), unit)] = source[dy]
    width = q_out.shape[0]
    cut = k_out.shape[0]
    base = 0

    def section(rows, cols):
        nonlocal base
        count = -(-cols // LANES)
        parts = [held[base + i * rows : base + (i + 1) * rows] for i in range(count)]
        base += count * rows
        return jnp.concatenate(parts, axis=1)[:, :cols].astype(f32)

    query = section(width, width)
    key = section(cut, width)
    value = flip(section(width, 2 * cut - LANES))[cut - LANES :]
    q_out[...] = query
    k_out[...] = key
    v_out[...] = value
    o_out[...] = section(width, width)
    gain_two[...] = section(16, width)[0]
    total = jnp.sum(query * wq[...].astype(f32), axis=1, keepdims=True) / gain[...].astype(f32)
    total = flip(jnp.broadcast_to(total, (width, LANES)))[0:1]
    rest = jnp.sum(key * wk[...].astype(f32), axis=0, keepdims=True)
    rest = rest + jnp.sum(value * wv[...].astype(f32), axis=0, keepdims=True)
    line = flip(jnp.broadcast_to(gain[...].astype(f32), (width, LANES)))[0:1]
    gain_one[...] = (total + rest / line)[0]


def unpack_main_kernel(other, *refs):
    pieces = refs[:SIDE]
    gate, up, down, held, wide, sems = refs[-6:]
    unit = pieces[0].shape[0]
    part = unit // 2
    for k in range(SIDE):
        place = lax.rem(lax.axis_index("y") - k + SIDE, SIDE)
        for index in range(2):
            span = pl.ds(pl.multiple_of(place * part, 16), part)
            held[index, span] = pieces[k][index * part : (index + 1) * part]
    core = lax.axis_index("core")
    core = 1 - core if other else core
    width, cols = wide.shape[1:]
    copies = []
    for k, target in enumerate((gate, up, down)):
        for t in range(cols // LANES):
            per = CHUNK // LANES
            base = (t % per * 3 + k) * width
            wide[k, :, t * LANES : (t + 1) * LANES] = held[t // per, base : base + width].astype(f32)
        span = pl.ds(pl.multiple_of(core * cols, LANES), cols)
        copies.append(pltpu.make_async_copy(wide.at[k], target.at[:, span], sems.at[k]))
        copies[-1].start()
    for copy in copies:
        copy.wait()


def unpack_main(pieces, width, hidden, filled):
    unit = pieces[0].shape[0]
    outs = [shape_of((width, hidden), f32)] * 3
    return pl.pallas_call(
        functools.partial(unpack_main_kernel, filled is not None),
        in_specs=[VMEM] * SIDE + ([ANY] * 3 if filled else []),
        out_specs=[ANY] * 3,
        out_shape=outs,
        scratch_shapes=[
            pltpu.VMEM((2, SIDE * unit // 2, LANES), bf16),
            pltpu.VMEM((3, width, hidden // 2), f32),
            pltpu.SemaphoreType.DMA((3,)),
        ],
        input_output_aliases={SIDE + i: i for i in range(3)} if filled else {},
        compiler_params=params(),
        cost_estimate=cost(1.5),
        name="unpack_main",
    )(*pieces, *(filled or ()))


def shift(value, axis, distance):
    size = lax.axis_size(axis)
    return lax.ppermute(value, axis, [(i, (i + distance) % size) for i in range(size)])


def mirror(value):
    size = SIDE * SIDE
    return lax.ppermute(value, SEQ, [(i, size - 1 - i) for i in range(size)])


def collect(value, axis):
    return [value] + [shift(value, axis, k) for k in range(1, SIDE)]


def exchange(parts, axis):
    total = parts[0].astype(f32)
    for k in range(1, SIDE):
        total = total + shift(parts[k], axis, k).astype(f32)
    return total


def scatter_parts(held, axis):
    rows, lanes = held.shape
    places = lax.axis_size(axis)
    return lax.all_to_all(held.reshape(places, rows // places, lanes), axis, 0, 0)


def sum_parts(parts):
    return jnp.sum(parts.astype(f32), axis=0).astype(bf16)


def scatter_sum(held, axis):
    return sum_parts(scatter_parts(held, axis))


def gather_all(held, axis):
    rows, lanes = held.shape
    places = lax.axis_size(axis)
    spread = jnp.broadcast_to(held[None], (places,) + held.shape)
    return lax.all_to_all(spread, axis, 0, 0).reshape(places * rows, lanes)


def after(value, *others):
    return lax.optimization_barrier((value, *others))[0]


def per_device(
    tokens,
    doc_lengths,
    second_query,
    second_grad,
    out_grad,
    first_gain,
    query_weight,
    key_weight,
    value_weight,
    output_weight,
    second_gain,
    gate_weight,
    up_weight,
    down_weight,
):
    micro, rows, width = tokens.shape
    kwidth = key_weight.shape[1]
    total = micro * rows
    tiles = -(-width // LANES)
    core = lax.axis_index("core").reshape(1)
    tokens, second_query, second_grad, out_grad = (
        jnp.swapaxes(v, 1, 2) for v in (tokens, second_query, second_grad, out_grad)
    )
    wk, wv, wd = key_weight.T, value_weight.T, down_weight.T
    gain_one, gain_two = first_gain.reshape(width, 1), second_gain.reshape(width, 1)

    table = shape_of((HALF, total), f32)
    start = shape_of((micro, 1, rows), jnp.int32)
    normed, kv, cosine, sine, starts, far_starts = simple(
        prepare_kernel,
        [SMEM] + [VMEM] * 4,
        [
            shape_of((micro, width + 4 * HALF, rows), bf16),
            shape_of((micro, rows, 2 * kwidth), bf16),
            table,
            table,
            start,
            start,
        ],
        (doc_lengths, tokens, gain_one, wk, wv),
        "prepare",
    )
    kv = lax.all_gather(kv, SEQ, axis=0)
    (q1,) = simple(
        query_kernel,
        [VMEM] * 4,
        [shape_of((micro, width, rows), bf16)],
        (normed, query_weight, cosine, sine),
        "query",
    )
    kv, q1, second_query, second_grad, gathered = lax.optimization_barrier(
        (kv, q1, second_query, second_grad, normed)
    )
    gathered = lax.all_gather(gathered, SEQ, axis=0)
    far_query, far_grad = mirror(second_query), mirror(second_grad)
    first_low, first_flat, first_lse = attend_forward(False, kv, q1, starts)
    first_low, far_query = lax.optimization_barrier((first_low, far_query))
    ffn_args = (first_low, tokens, output_weight, gain_two, out_grad, gate_weight, up_weight, wd)
    away, *before = feed_forward(core, *ffn_args, ())
    far_query = after(far_query, away)
    _, second_flat, second_lse = attend_forward(True, kv, far_query, far_starts)
    received, second_lse = lax.optimization_barrier((shift(away, "core", 1), second_lse))
    result, main0, main1, middle_grad, d1, gain_two_grad, wo_grad = feed_forward(core, *ffn_args, (*before, received))
    main0 = scatter_parts(main0, "y")
    kv_grad, query_grad, second_query_grad = attend_backward(
        kv,
        q1,
        far_query,
        d1,
        far_grad,
        first_flat,
        second_flat,
        first_lse,
        second_lse,
        starts,
        far_starts,
        cosine,
        sine,
    )
    kv_grad, gathered = lax.optimization_barrier((kv_grad, gathered))
    wk_grad, wv_grad = simple(
        kv_weights_kernel,
        [VMEM] * 4,
        [shape_of((kwidth, width), f32), shape_of((width, 2 * kwidth - LANES), f32)],
        (after(kv_grad, main0), gathered, starts, far_starts),
        "kv_weights",
    )
    main1 = scatter_parts(after(main1, main0), "y")
    kv_grad = lax.psum_scatter(kv_grad.reshape(-1, 2 * kwidth), SEQ, scatter_dimension=0, tiled=True)
    half = tail_rows(width)
    tail_half = shape_of((SIDE, half // SIDE, LANES), bf16)
    normed_part, tail, tail_away = pl.pallas_call(
        query_back_kernel,
        in_specs=[VMEM] * 7,
        out_specs=[VMEM] * 3,
        out_shape=[shape_of((width, total), f32), tail_half, tail_half],
        scratch_shapes=[pltpu.VMEM((2 * half, LANES), bf16)],
        compiler_params=params(),
        cost_estimate=cost(1),
        name="query_back",
    )(normed, query_grad, query_weight, wk_grad, wv_grad, wo_grad, gain_two_grad)
    second_query_grad = mirror(second_query_grad)
    main1 = after(main1, normed_part)
    main = jnp.concatenate([sum_parts(main0), sum_parts(main1)], axis=0)
    main = scatter_parts(main, SEQ)
    tail = (tail.astype(f32) + shift(tail_away, "core", 1).astype(f32)).astype(bf16)
    tail = exchange([tail[k] for k in range(SIDE)], "y").astype(bf16)
    tail, main = lax.optimization_barrier((tail, main))
    main = gather_all(sum_parts(main), SEQ)
    main = collect(main, "y")
    tail = gather_all(scatter_sum(tail, SEQ), SEQ)
    tail, main = lax.optimization_barrier((tail, main))
    hidden = gate_weight.shape[1]
    main_away = [shift(v, "core", 1) for v in main]
    filled = unpack_main(main, width, hidden, None)
    tail, filled = lax.optimization_barrier((collect(tail, "y"), filled))
    tail = jnp.stack(tail)
    tail_away = shift(tail, "core", 1)
    gate, up, down = unpack_main(main_away, width, hidden, filled)
    tokens_like = shape_of((micro, width, rows), bf16)
    input_grad, second_query_grad = simple(
        input_back_kernel,
        [VMEM] * 10,
        [tokens_like, tokens_like],
        (kv_grad, wk, wv, cosine, sine, normed_part, tokens, gain_one, middle_grad, second_query_grad),
        "input_back",
    )
    square = shape_of((width, width), f32)
    narrow = shape_of((kwidth, width), f32)
    line = shape_of((width,), f32)
    q_total, k_total, v_total, o_total, gain_one_total, gain_two_total = pl.pallas_call(
        unpack_tail_kernel,
        in_specs=[VMEM] * 6,
        out_specs=[VMEM] * 6,
        out_shape=[square, narrow, narrow, square, line, line],
        scratch_shapes=[pltpu.VMEM((2 * half, LANES), bf16)],
        compiler_params=params(),
        cost_estimate=cost(1),
        name="unpack_tail",
    )(tail, tail_away, query_weight, wk, wv, gain_one)
    return (
        jnp.swapaxes(result, 1, 2),
        jnp.swapaxes(input_grad, 1, 2),
        jnp.swapaxes(second_query_grad, 1, 2),
        gain_one_total,
        q_total,
        k_total.T,
        v_total.T,
        o_total,
        gain_two_total,
        gate,
        up,
        down.T,
    )


def exchange_all(value, axis):
    return [value.astype(f32)] + [shift(value, axis, k).astype(f32) for k in range(1, SIDE)]


def solution(mesh):
    grid = Mesh(mesh.devices.reshape(SIDE, SIDE, SIDE, 2), ("z", "x", "y", "core"))
    split = P(("y", "core"), SEQ, None)
    in_specs = (split, P(("y", "core"), None), split, split, split) + (P(),) * 9
    out_specs = (split, split, split) + (P(),) * 9
    return jax.shard_map(
        per_device, mesh=grid, in_specs=in_specs, out_specs=out_specs, check_vma=False
    )
```

```python
import functools
import math

import jax
import jax.numpy as jnp
from jax import lax
from jax.experimental import pallas as pl
from jax.experimental.pallas import tpu as pltpu
from jax.sharding import Mesh
from jax.sharding import PartitionSpec as P

HEADS = 9
KVH = 3
HD = 64
HALF = HD // 2
GROUP = HEADS // KVH
NEGATIVE = -1e30
EPSILON = 1e-05
ROPE_BASE = 100000.0
FACTOR = 1.0 / math.sqrt(HD)
LANES = 128
SIDE = 4
KEYS = 256
CHUNK = 256
SEQ = ("z", "x")
SIMPLE = {"kv_weights": 2.0, "input_back": 1.0, "prepare": 1.0, "query": 1.0}
f32 = jnp.float32
bf16 = jnp.bfloat16

VMEM = pl.BlockSpec(memory_space=pltpu.VMEM)
SMEM = pl.BlockSpec(memory_space=pltpu.SMEM)


def cost(microseconds):
    return pl.CostEstimate(flops=int(microseconds * 10**9), bytes_accessed=1000, transcendentals=0)


ANY = pl.BlockSpec(memory_space=pl.ANY)


def params(megabytes=56):
    return pltpu.CompilerParams(vmem_limit_bytes=megabytes * 1024 * 1024)


def shape_of(dims, dtype):
    return jax.ShapeDtypeStruct(dims, dtype)


def mul(left, right):
    return lax.dot_general(left, right, (((1,), (0,)), ((), ())), preferred_element_type=f32)


def mul_nt(left, right):
    return lax.dot_general(left, right, (((1,), (1,)), ((), ())), preferred_element_type=f32)


def flip(array):
    rows, cols = array.shape
    spare = -cols % LANES
    if spare:
        array = jnp.concatenate([array, jnp.zeros((rows, spare), array.dtype)], axis=1)
    extra = -rows % LANES
    if extra:
        array = jnp.concatenate([array, jnp.zeros((extra, cols + spare), array.dtype)], axis=0)
    return jnp.transpose(array)[:cols, :rows]


def side_by_side(ref):
    return jnp.concatenate([ref[m] for m in range(ref.shape[0])], axis=1)


def interleave(keys, values):
    parts = []
    for g in range(KVH):
        span = slice(g * HD, (g + 1) * HD)
        parts += [keys[span], values[span]]
    return jnp.concatenate(parts, axis=0)


def part_of(flat, index):
    return jnp.concatenate(
        [flat[(2 * g + index) * HD : (2 * g + index + 1) * HD] for g in range(KVH)], axis=0
    )


def own_block():
    return lax.axis_index("z") * SIDE + lax.axis_index("x")


def far_block():
    return SIDE * SIDE - 1 - own_block()


def turn(flat, cosine, sine, heads):
    parts = []
    for head in range(heads):
        front = flat[head * HD : head * HD + HALF]
        back = flat[head * HD + HALF : (head + 1) * HD]
        parts += [front * cosine - back * sine, back * cosine + front * sine]
    return parts


def simple(kernel, in_specs, outs, args, name):
    return pl.pallas_call(
        kernel,
        in_specs=in_specs,
        out_specs=[VMEM] * len(outs),
        out_shape=outs,
        compiler_params=params(),
        cost_estimate=cost(SIMPLE[name]),
        name=name,
    )(*args)


def prepare_kernel(lengths, tokens, gain, wk, wv, normed_out, kv_out, cos_out, sin_out, starts, far_starts):
    micro, _, rows = tokens.shape
    lane = lax.broadcasted_iota(jnp.int32, (1, rows), 1)
    places = own_block() * rows + lane
    far_places = far_block() * rows + lane
    positions = []
    for m in range(micro):
        start = jnp.zeros((1, rows), jnp.int32)
        far = jnp.zeros((1, rows), jnp.int32)
        end = jnp.int32(0)
        for j in range(lengths.shape[1]):
            length = lengths[m, j]
            end = end + length
            start = start + jnp.where(places >= end, length, 0)
            far = far + jnp.where(far_places >= end, length, 0)
        starts[m] = start
        far_starts[m] = far
        positions.append(places - start)
    order = lax.broadcasted_iota(jnp.int32, (HALF, micro * rows), 0).astype(f32)
    frequency = jnp.exp(order * (-2.0 * math.log(ROPE_BASE) / HD))
    angles = jnp.concatenate(positions, axis=1).astype(f32) * frequency
    cosine, sine = jnp.cos(angles), jnp.sin(angles)
    cos_out[...] = cosine
    sin_out[...] = sine
    inputs = side_by_side(tokens).astype(f32)
    scale = lax.rsqrt(jnp.mean(inputs * inputs, axis=0, keepdims=True) + EPSILON)
    normed = (inputs * scale * gain[...].astype(f32)).astype(bf16)
    width = tokens.shape[1]
    for m in range(micro):
        span = slice(m * rows, (m + 1) * rows)
        normed_out[m, :width] = normed[:, span]
        base = width
        for table in (cosine, sine):
            high = table[:, span].astype(bf16)
            normed_out[m, base : base + HALF] = high
            normed_out[m, base + HALF : base + 2 * HALF] = (table[:, span] - high.astype(f32)).astype(bf16)
            base += 2 * HALF
    keys = turn(mul(wk[...], normed), cosine, sine, KVH)
    flat = interleave(jnp.concatenate(keys, axis=0), mul(wv[...], normed)).astype(bf16)
    for m in range(micro):
        kv_out[m] = flip(flat[:, m * rows : (m + 1) * rows])


def query_kernel(normed, weight, cos_ref, sin_ref, q1_out):
    width = weight.shape[0]
    flat = mul(flip(weight[...]), jnp.concatenate([normed[m, :width] for m in range(normed.shape[0])], axis=1))
    parts = turn(flat, cos_ref[...], sin_ref[...], HEADS)
    turned = (jnp.concatenate(parts, axis=0).astype(bf16) * FACTOR).astype(bf16)
    rows = q1_out.shape[2]
    for m in range(q1_out.shape[0]):
        q1_out[m] = turned[:, m * rows : (m + 1) * rows]


def lane_heads(ref, group):
    return jnp.concatenate(
        [ref[(group * GROUP + h) * HD : (group * GROUP + h + 1) * HD, :] for h in range(GROUP)], axis=1
    )


def visible_bias(start, block, first_key, rows):
    keys = first_key + lax.broadcasted_iota(jnp.int32, (KEYS, rows), 0)
    queries = block * rows + lax.broadcasted_iota(jnp.int32, (KEYS, rows), 1)
    seen = (keys >= start) & (keys <= queries)
    bias = jnp.where(seen, 0.0, NEGATIVE)
    return jnp.concatenate([bias] * GROUP, axis=1)


def key_steps(start, block, rows):
    per = KEYS // rows
    return jnp.min(start) // KEYS, block // per + 1


def forward_kernel(far, held, query_ref, starts, low_out, flat_out, lse_out, acc, peak, mass, query):
    block_place = far_block() if far else own_block()
    scale = FACTOR if far else 1.0
    query[...] = (query_ref[0] * scale).astype(bf16)
    rows = query.shape[1]
    per = KEYS // rows
    acc[...] = jnp.zeros_like(acc)
    peak[...] = jnp.full_like(peak, NEGATIVE)
    mass[...] = jnp.zeros_like(mass)
    start = starts[0]
    first_step, last_step = key_steps(start, block_place, rows)

    @pl.loop(first_step, last_step)
    def _(step):
        block = held[pl.ds(step * per, per), 0].reshape(KEYS, held.shape[3])
        bias = visible_bias(start, block_place, step * KEYS, rows)
        tiles = [block[:, i * LANES : (i + 1) * LANES] for i in range(3)]
        for g in range(KVH):
            heads = lane_heads(query, g)
            scores = mul(tiles[g], jnp.concatenate([heads, jnp.zeros_like(heads)], axis=0)) + bias
            old = peak[g]
            top = jnp.maximum(old, jnp.max(scores, axis=0, keepdims=True))
            weights = jnp.exp(scores - top)
            decay = jnp.exp(old - top)
            values = jnp.transpose(tiles[g])[HD:]
            mass[g] = mass[g] * decay + jnp.sum(weights, axis=0, keepdims=True)
            acc[g] = acc[g] * decay + mul(values, weights.astype(bf16))
            peak[g] = top

    for g in range(KVH):
        lse_out[0, g] = peak[g] + jnp.log(mass[g])
        result = acc[g] * (1.0 / mass[g])
        for h in range(GROUP):
            head = g * GROUP + h
            flat_out[0, head * HD : (head + 1) * HD, :] = result[:, h * rows : (h + 1) * rows]
    low_out[...] = flat_out[...].astype(bf16)


def one_of(dims, axis=0):
    block = tuple(1 if i == axis else n for i, n in enumerate(dims))
    return pl.BlockSpec(block, lambda m: tuple(m if i == axis else 0 for i in range(len(dims))))


def attend_forward(far, kv, query, starts):
    micro, width, rows = query.shape
    lanes = GROUP * rows
    low = shape_of(query.shape, bf16)
    flat = shape_of(query.shape, f32)
    lse = shape_of((micro, KVH, 1, lanes), f32)
    return pl.pallas_call(
        functools.partial(forward_kernel, far),
        grid=(micro,),
        in_specs=[one_of(kv.shape, 1), one_of(query.shape), one_of(starts.shape)],
        out_specs=[one_of(v.shape) for v in (low, flat, lse)],
        out_shape=[low, flat, lse],
        scratch_shapes=[
            pltpu.VMEM((KVH, HD, lanes), f32),
            pltpu.VMEM((KVH, 1, lanes), f32),
            pltpu.VMEM((KVH, 1, lanes), f32),
            pltpu.VMEM((width, rows), bf16),
        ],
        compiler_params=params(),
        cost_estimate=cost(2.5),
        name="attention_forward",
    )(kv, query, starts)


def backward_kernel(
    held, q1_ref, q2_ref, d1_ref, d2_ref, o1, o2, lse1, lse2, starts, far_starts, cos_ref, sin_ref,
    kv_out, first_grad, second_grad, sums, delta, dq, query2, both,
):
    rows = q1_ref.shape[2]
    per = KEYS // rows
    query2[...] = (q2_ref[0] * FACTOR).astype(bf16)
    sums[...] = jnp.zeros_like(sums)
    dq[...] = jnp.zeros_like(dq)

    def attention(a, q_ref, d_ref, o_ref, lse_ref, start, block_place):
        for g in range(KVH):
            query, grad = lane_heads(q_ref, g), lane_heads(d_ref, g)
            delta[a, g] = jnp.sum(grad.astype(f32) * lane_heads(o_ref, g), axis=0, keepdims=True)
            zero = jnp.zeros_like(query)
            both[g] = jnp.concatenate(
                [jnp.concatenate([query, zero], axis=1), jnp.concatenate([zero, grad], axis=1)], axis=0
            )
        first_step, last_step = key_steps(start, block_place, rows)

        @pl.loop(first_step, last_step)
        def _(step):
            block = held[pl.ds(step * per, per), 0].reshape(KEYS, held.shape[3])
            bias = visible_bias(start, block_place, step * KEYS, rows)
            tiles = [block[:, i * LANES : (i + 1) * LANES] for i in range(3)]
            total = []
            for g in range(KVH):
                pair = both[g]
                lanes = pair.shape[1] // 2
                products = mul(tiles[g], pair)
                weights = jnp.exp(products[:, :lanes] + bias - lse_ref[0, g])
                score_grad = (weights * (products[:, lanes:] - delta[a, g])).astype(bf16)
                dq[a, g] += mul(jnp.transpose(tiles[g])[:HD], score_grad)
                total.append(mul_nt(jnp.concatenate([score_grad, weights.astype(bf16)], axis=1), pair))
            joined = jnp.concatenate(total, axis=1)
            sums[pl.ds(step * per, per)] += joined.reshape(per, rows, joined.shape[1])

    attention(0, q1_ref.at[0], d1_ref.at[0], o1.at[0], lse1, starts[0], own_block())
    attention(1, query2, d2_ref.at[0], o2.at[0], lse2, far_starts[0], far_block())
    kv_out[:, 0] = sums[...].astype(bf16)
    cosine, sine = cos_ref[...], -sin_ref[...]
    for g in range(KVH):
        for h in range(GROUP):
            head = g * GROUP + h
            lanes = slice(h * rows, (h + 1) * rows)
            target = slice(head * HD, (head + 1) * HD)
            parts = turn(dq[0, g][:, lanes] * FACTOR, cosine, sine, 1)
            first_grad[0, target, :] = jnp.concatenate(parts, axis=0).astype(bf16)
            second_grad[0, target, :] = (dq[1, g][:, lanes] * FACTOR).astype(bf16)


def attend_backward(kv, *arrays):
    micro, width, rows = arrays[0].shape
    lanes = GROUP * rows
    blocks, _, _, kv_width = kv.shape
    part = shape_of((micro, width, rows), bf16)
    table = pl.BlockSpec((HALF, rows), lambda m: (0, m))
    return pl.pallas_call(
        backward_kernel,
        grid=(micro,),
        in_specs=[one_of(kv.shape, 1)] + [one_of(v.shape) for v in arrays[:-2]] + [table] * 2,
        out_specs=[one_of(kv.shape, 1)] + [one_of(part.shape)] * 2,
        out_shape=[shape_of(kv.shape, bf16), part, part],
        scratch_shapes=[
            pltpu.VMEM((blocks, rows, kv_width), f32),
            pltpu.VMEM((2, KVH, 1, lanes), f32),
            pltpu.VMEM((2, KVH, HD, lanes), f32),
            pltpu.VMEM((width, rows), bf16),
            pltpu.VMEM((KVH, 2 * HD, 2 * lanes), bf16),
        ],
        compiler_params=params(),
        cost_estimate=cost(7),
        name="attention_backward",
    )(kv, *arrays)


def weights_kernel(
    sums, normed, starts, far_starts, own_normed, grad_ref, weight, wo_grad, gain_two_grad,
    normed_grad, kept, away, kv_out, packed,
):
    rows = starts.shape[2]
    width = weight.shape[0]
    per = KEYS // rows

    @pl.when(pl.program_id(0) == 0)
    def _():
        kv_out[...] = jnp.zeros_like(kv_out)

    def add(step):
        block = sums[pl.ds(step * per, per), 0].reshape(KEYS, sums.shape[3])
        inner = [normed[step * per + i, 0] for i in range(per)]
        values = jnp.concatenate([v[:width] for v in inner], axis=1)
        tables = jnp.concatenate([v[width:] for v in inner], axis=1).astype(f32)
        cosine = tables[:HALF] + tables[HALF : 2 * HALF]
        sine = tables[2 * HALF : 3 * HALF] + tables[3 * HALF :]
        flat = jnp.concatenate([jnp.transpose(block[:, g * LANES : (g + 1) * LANES]) for g in range(KVH)], axis=0)
        keys = turn(part_of(flat, 0).astype(f32), cosine, -sine, KVH)
        both = jnp.concatenate([jnp.concatenate(keys, axis=0).astype(bf16), part_of(flat, 1)], axis=0)
        kv_out[...] += mul_nt(both, values)

    near = key_steps(starts[0], own_block(), rows)
    far = key_steps(far_starts[0], far_block(), rows)
    pl.loop(*near)(add)

    @pl.loop(*far)
    def _(step):
        pl.when((step < near[0]) | (step >= near[1]))(lambda: add(step))


    @pl.when(pl.program_id(0) == pl.num_programs(0) - 1)
    def _():
        grad = side_by_side(grad_ref)
        values = jnp.concatenate([own_normed[m, :width] for m in range(own_normed.shape[0])], axis=1)
        normed_grad[...] = mul(weight[...], grad)
        lane = lax.broadcasted_iota(jnp.int32, (width, LANES), 1)
        gains = flip(jnp.where(lane == 0, gain_two_grad[...], 0.0))[:16]
        base = 0
        for array in (mul_nt(values, grad), kv_out[...], wo_grad[...], gains):
            base = pack_rows(packed, base, array.astype(bf16))
        packed[base:] = jnp.zeros((packed.shape[0] - base, LANES), bf16)
        unit = kept.shape[1]
        for dy in range(SIDE):
            for target, dc in ((kept, 0), (away, 1)):
                target[dy] = packed[pl.ds(pl.multiple_of(place_of(dc, dy, 1) * unit, 16), unit)]


def weights_back(sums, normed, starts, far_starts, *others):
    micro, _, rows = starts.shape
    width = others[2].shape[0]
    kv_width = sums.shape[3]
    unit = tail_rows(width)
    tail = shape_of((SIDE, unit, LANES), bf16)
    outs = [shape_of((width, micro * rows), f32), tail, tail]

    def whole(v):
        return pl.BlockSpec(v.shape, lambda m: (0,) * len(v.shape))

    return pl.pallas_call(
        weights_kernel,
        grid=(micro,),
        in_specs=[one_of(sums.shape, 1), one_of(normed.shape, 1), one_of(starts.shape), one_of(starts.shape)]
        + [whole(v) for v in others],
        out_specs=[whole(v) for v in outs],
        out_shape=outs,
        scratch_shapes=[
            pltpu.VMEM((kv_width, width), f32),
            pltpu.VMEM((2 * SIDE * unit, LANES), bf16),
        ],
        compiler_params=params(),
        cost_estimate=cost(3),
        name="weights_back",
    )(sums, normed, starts, far_starts, *others)


def norm_back(vector, scale, gain, gradient):
    weighted = gradient * gain
    gain_grad = jnp.sum(gradient * vector * scale, axis=1, keepdims=True)
    inner = jnp.mean(weighted * vector, axis=0, keepdims=True)
    return scale * weighted - vector * (scale * scale * scale * inner), gain_grad


def ffn_kernel(
    last, core, first, tokens, out_weight, gain, out_grad, wg, wu, wd, *refs,
):
    step = pl.program_id(0)
    micro, width, rows = tokens.shape
    if last:
        before, result_before, grad_before, received = refs[:4]
        result, main, middle_grad, d1, gain_grad, wo_grad = refs[4:10]
        normed, normed_t, grad, grad_t, result_sum, normed_grad = refs[10:]
        middle = before
    else:
        main, middle, result_sum, normed_grad = refs[:4]
        normed, normed_t, grad, grad_t = refs[4:]

    @pl.when(step == 0)
    def _():
        if last:
            value = before[...]
            result_sum[...] = result_before[...]
            normed_grad[...] = grad_before[...]
        else:
            value = side_by_side(tokens).astype(f32) + mul(flip(out_weight[...]), side_by_side(first))
            middle[...] = value
            result_sum[...] = jnp.zeros_like(result_sum)
            normed_grad[...] = jnp.zeros_like(normed_grad)
        scale = lax.rsqrt(jnp.mean(value * value, axis=0, keepdims=True) + EPSILON)
        low = (value * scale * gain[...].astype(f32)).astype(bf16)
        normed_t[...] = low
        normed[...] = flip(low)
        flat = side_by_side(out_grad)
        grad_t[...] = flat
        grad[...] = flip(flat)

    low = normed[...]
    gate = mul(low, wg[...])
    up = mul(low, wu[...])
    sigmoid = 1.0 / (1.0 + jnp.exp(-gate))
    active = gate * sigmoid
    hidden = (active * up).astype(bf16)
    result_sum[...] += mul_nt(hidden, wd[...])
    hidden_grad = mul(grad[...], wd[...])
    gate_grad = (hidden_grad * up * sigmoid * (1.0 + gate * (1.0 - sigmoid))).astype(bf16)
    up_grad = (hidden_grad * active).astype(bf16)
    parts = (mul(normed_t[...], gate_grad), mul(normed_t[...], up_grad), mul(grad_t[...], hidden))
    for i in range(CHUNK // LANES):
        span = slice(i * LANES, (i + 1) * LANES)
        for k, part in enumerate(parts):
            rows_at = slice((i * 3 + k) * width, (i * 3 + k + 1) * width)
            value = part[:, span].astype(bf16)
            if last:
                value = (value.astype(f32) + received[rows_at].astype(f32)).astype(bf16)
            main[rows_at] = value
    normed_grad[...] += mul_nt(gate_grad, wg[...]) + mul_nt(up_grad, wu[...])
    if not last:
        return

    @pl.when(step == pl.num_programs(0) - 1)
    def _():
        value = middle[...]
        final = (value + flip(result_sum[...])).astype(bf16)
        scale = lax.rsqrt(jnp.mean(value * value, axis=0, keepdims=True) + EPSILON)
        part, gains = norm_back(value, scale, gain[...].astype(f32), flip(normed_grad[...]))
        gain_grad[...] = gains
        total = grad_t[...].astype(f32) + part
        middle_grad[...] = total
        branch = total.astype(bf16)
        wo_grad[...] = mul_nt(side_by_side(first), branch).astype(bf16)
        back = mul(out_weight[...], branch).astype(bf16)
        for m in range(micro):
            span = slice(m * rows, (m + 1) * rows)
            d1[m] = back[:, span]
            result[m] = final[:, span]


def pack_rows(target, base, array):
    rows, cols = array.shape
    for i in range(-(-cols // LANES)):
        span = array[:, i * LANES : (i + 1) * LANES]
        if span.shape[1] < LANES:
            span = jnp.concatenate([span, jnp.zeros((rows, LANES - span.shape[1]), span.dtype)], axis=1)
        target[base : base + rows] = span
        base += rows
    return base


def main_rows(width, hidden):
    used = hidden // 2 // LANES * 3 * width
    unit = SIDE * SIDE * SIDE * 8
    return -(-used // unit) * unit


def feed_forward(core, first, tokens, out_weight, gain, out_grad, wg, wu, wd, before):
    micro, width, rows = tokens.shape
    total = micro * rows
    hidden = wg.shape[1]
    steps = hidden // 2 // CHUNK
    block = pl.BlockSpec((CHUNK // LANES * 3 * width, LANES), lambda i, c: (i, 0))
    last = len(before) > 0

    def whole(*dims):
        return pl.BlockSpec(dims, lambda i, c: (0,) * len(dims))

    def column(i, c):
        side = c[0] if last else 1 - c[0]
        return (0, side * steps + i)

    weight = pl.BlockSpec((width, CHUNK), column)
    flat, natural = shape_of((width, total), f32), shape_of((total, width), f32)
    spec, tall = whole(width, total), whole(total, width)
    token_spec, token_shape = whole(micro, width, rows), shape_of((micro, width, rows), bf16)
    if last:
        outs = [
            (token_shape, token_spec),
            (shape_of((main_rows(width, hidden), LANES), bf16), block),
            (flat, spec),
            (token_shape, token_spec),
            (shape_of((width, 1), f32), whole(width, 1)),
            (shape_of((width, width), bf16), whole(width, width)),
        ]
        more = [spec, tall, tall, block]
        scratch = [pltpu.VMEM((total, width), f32)] * 2
    else:
        outs = [
            (shape_of((hidden // 2 // LANES * 3 * width, LANES), bf16), block),
            (flat, spec),
            (natural, tall),
            (natural, tall),
        ]
        more, scratch = [], []
    low = [pltpu.VMEM((total, width), bf16), pltpu.VMEM((width, total), bf16)]
    return pl.pallas_call(
        functools.partial(ffn_kernel, last),
        grid_spec=pltpu.PrefetchScalarGridSpec(
            num_scalar_prefetch=1,
            grid=(steps,),
            in_specs=[
                token_spec,
                token_spec,
                whole(width, width),
                whole(width, 1),
                token_spec,
                weight,
                weight,
                weight,
            ]
            + more,
            out_specs=[v[1] for v in outs],
            scratch_shapes=low * 2 + scratch,
        ),
        out_shape=[v[0] for v in outs],
        compiler_params=params(),
        cost_estimate=cost(3),
        name="feed_forward",
    )(core, first, tokens, out_weight, gain, out_grad, wg, wu, wd, *before)


def tail_rows(width):
    tiles = -(-width // LANES)
    used = tiles * (2 * width + 2 * KVH * HD + 16)
    unit = 2 * SIDE * SIDE * SIDE * 8
    return -(-used // unit) * (unit // 2 // SIDE)


def place_of(dc, dy, sign):
    cc = lax.rem(lax.axis_index("core") + dc, 2)
    yy = lax.rem(lax.axis_index("y") + sign * dy + SIDE, SIDE)
    return cc * SIDE + yy


def input_back_kernel(
    kv_grad, wk, wv, cos_ref, sin_ref, partial, tokens, gain, middle_grad, second, input_grad, second_grad
):
    second_grad[...] = second[...]
    micro, width, rows = tokens.shape
    flat = jnp.concatenate(
        [flip(kv_grad[m * rows : (m + 1) * rows].astype(f32)) for m in range(micro)], axis=1
    )
    parts = turn(part_of(flat, 0), cos_ref[...], -sin_ref[...], KVH)
    low = jnp.concatenate(parts + [part_of(flat, 1)], axis=0).astype(bf16)
    weights = flip(jnp.concatenate([wk[...], wv[...]], axis=0))
    normed_grad = partial[...] + mul(weights, low)
    inputs = side_by_side(tokens).astype(f32)
    scale = lax.rsqrt(jnp.mean(inputs * inputs, axis=0, keepdims=True) + EPSILON)
    part, _ = norm_back(inputs, scale, gain[...].astype(f32), normed_grad)
    final = (middle_grad[...] + part).astype(bf16)
    for m in range(micro):
        input_grad[m] = final[:, m * rows : (m + 1) * rows]


def unpack_tail_kernel(kept, away, wq, wk, wv, gain, q_out, k_out, v_out, o_out, gain_one, gain_two, held):
    places, _, rows, _ = kept.shape
    for dy in range(SIDE):
        for source, dc in ((kept, 0), (away, 1)):
            base = place_of(dc, dy, -1) * places * rows
            for i in range(places):
                held[pl.ds(pl.multiple_of(base + i * rows, 16), rows)] = source[i, dy]
    width = q_out.shape[0]
    cut = k_out.shape[0]
    base = 0

    def section(rows, cols):
        nonlocal base
        count = -(-cols // LANES)
        parts = [held[base + i * rows : base + (i + 1) * rows] for i in range(count)]
        base += count * rows
        return jnp.concatenate(parts, axis=1)[:, :cols].astype(f32)

    query = section(width, width)
    both = section(2 * cut, width)
    key, value = both[:cut], both[cut:]
    q_out[...] = query
    k_out[...] = key
    v_out[...] = value
    o_out[...] = section(width, width)
    gain_two[...] = section(16, width)[0]
    total = jnp.sum(query * wq[...].astype(f32), axis=1, keepdims=True) / gain[...].astype(f32)
    total = flip(jnp.broadcast_to(total, (width, LANES)))[0:1]
    rest = jnp.sum(key * wk[...].astype(f32), axis=0, keepdims=True)
    rest = rest + jnp.sum(value * wv[...].astype(f32), axis=0, keepdims=True)
    line = flip(jnp.broadcast_to(gain[...].astype(f32), (width, LANES)))[0:1]
    gain_one[...] = (total + rest / line)[0]


def unpack_main_kernel(other, *refs):
    pieces = refs[: SIDE + 1]
    gate, up, down, held, wide, sems = refs[-6:]
    unit = pieces[0].shape[0]
    half = unit // 2
    for k, offset, piece in zip((0, 1, 2, 2, 3), (0, 0, 0, half, 0), pieces):
        place = lax.rem(lax.axis_index("y") - k + SIDE, SIDE)
        held[pl.ds(pl.multiple_of(place * unit + offset, 16), piece.shape[0])] = piece[...]
    core = lax.axis_index("core")
    core = 1 - core if other else core
    width, cols = wide.shape[1:]
    copies = []
    for k, target in enumerate((gate, up, down)):
        for t in range(cols // LANES):
            base = (t * 3 + k) * width
            wide[k, :, t * LANES : (t + 1) * LANES] = held[base : base + width].astype(f32)
        span = pl.ds(pl.multiple_of(core * cols, LANES), cols)
        copies.append(pltpu.make_async_copy(wide.at[k], target.at[:, span], sems.at[k]))
        copies[-1].start()
    for copy in copies:
        copy.wait()


def unpack_main(pieces, width, hidden, filled):
    unit = pieces[0].shape[0]
    outs = [shape_of((width, hidden), f32)] * 3
    return pl.pallas_call(
        functools.partial(unpack_main_kernel, filled is not None),
        in_specs=[VMEM] * len(pieces) + ([ANY] * 3 if filled else []),
        out_specs=[ANY] * 3,
        out_shape=outs,
        scratch_shapes=[
            pltpu.VMEM((SIDE * unit, LANES), bf16),
            pltpu.VMEM((3, width, hidden // 2), f32),
            pltpu.SemaphoreType.DMA((3,)),
        ],
        input_output_aliases={len(pieces) + i: i for i in range(3)} if filled else {},
        compiler_params=params(),
        cost_estimate=cost(1.5),
        name="unpack_main",
    )(*pieces, *(filled or ()))


def shift(value, axis, distance):
    size = lax.axis_size(axis)
    return lax.ppermute(value, axis, [(i, (i + distance) % size) for i in range(size)])


def mirror(value):
    size = SIDE * SIDE
    return lax.ppermute(value, SEQ, [(i, size - 1 - i) for i in range(size)])


def collect(value, axis):
    return [value] + [shift(value, axis, k) for k in range(1, SIDE)]


def exchange(parts, axis):
    total = parts[0].astype(f32)
    for k in range(1, SIDE):
        total = total + shift(parts[k], axis, k).astype(f32)
    return total


def scatter_parts(held, axis):
    rows, lanes = held.shape
    places = lax.axis_size(axis)
    return lax.all_to_all(held.reshape(places, rows // places, lanes), axis, 0, 0)


def sum_parts(parts):
    return jnp.sum(parts.astype(f32), axis=0).astype(bf16)


def scatter_sum(held, axis):
    return sum_parts(scatter_parts(held, axis))


def gather_all(held, axis):
    rows, lanes = held.shape
    places = lax.axis_size(axis)
    spread = jnp.broadcast_to(held[None], (places,) + held.shape)
    return lax.all_to_all(spread, axis, 0, 0).reshape(places * rows, lanes)


def after(value, *others):
    return lax.optimization_barrier((value, *others))[0]


def per_device(
    tokens,
    doc_lengths,
    second_query,
    second_grad,
    out_grad,
    first_gain,
    query_weight,
    key_weight,
    value_weight,
    output_weight,
    second_gain,
    gate_weight,
    up_weight,
    down_weight,
):
    micro, rows, width = tokens.shape
    kwidth = key_weight.shape[1]
    total = micro * rows
    tiles = -(-width // LANES)
    core = lax.axis_index("core").reshape(1)
    tokens, second_query, second_grad, out_grad = (
        jnp.swapaxes(v, 1, 2) for v in (tokens, second_query, second_grad, out_grad)
    )
    wk, wv, wd = key_weight.T, value_weight.T, down_weight.T
    gain_one, gain_two = first_gain.reshape(width, 1), second_gain.reshape(width, 1)

    table = shape_of((HALF, total), f32)
    start = shape_of((micro, 1, rows), jnp.int32)
    normed, kv, cosine, sine, starts, far_starts = simple(
        prepare_kernel,
        [SMEM] + [VMEM] * 4,
        [
            shape_of((micro, width + 4 * HALF, rows), bf16),
            shape_of((micro, rows, 2 * kwidth), bf16),
            table,
            table,
            start,
            start,
        ],
        (doc_lengths, tokens, gain_one, wk, wv),
        "prepare",
    )
    kv = lax.all_gather(kv, SEQ, axis=0)
    (q1,) = simple(
        query_kernel,
        [VMEM] * 4,
        [shape_of((micro, width, rows), bf16)],
        (normed, query_weight, cosine, sine),
        "query",
    )
    far_query, far_grad = mirror(second_query), mirror(second_grad)
    kv, q1, far_query, far_grad, gathered = lax.optimization_barrier((kv, q1, far_query, far_grad, normed))
    gathered = lax.all_gather(gathered, SEQ, axis=0)
    first_low, first_flat, first_lse = attend_forward(False, kv, q1, starts)
    ffn_args = (first_low, tokens, output_weight, gain_two, out_grad, gate_weight, up_weight, wd)
    away, *before = feed_forward(core, *ffn_args, ())
    far_query = after(far_query, away)
    _, second_flat, second_lse = attend_forward(True, kv, far_query, far_starts)
    received, second_lse = lax.optimization_barrier((shift(away, "core", 1), second_lse))
    result, main, middle_grad, d1, gain_two_grad, wo_grad = feed_forward(core, *ffn_args, (*before, received))
    main = scatter_parts(main, "y")
    kv_grad, query_grad, second_query_grad = attend_backward(
        kv,
        q1,
        far_query,
        d1,
        far_grad,
        first_flat,
        second_flat,
        first_lse,
        second_lse,
        starts,
        far_starts,
        cosine,
        sine,
    )
    second_query_grad = mirror(second_query_grad)
    kv_grad, gathered, main, second_query_grad = lax.optimization_barrier((kv_grad, gathered, main, second_query_grad))
    main = scatter_parts(sum_parts(main), SEQ)
    normed_part, tail, tail_away = weights_back(
        kv_grad, gathered, starts, far_starts, normed, query_grad, query_weight, wo_grad, gain_two_grad
    )
    kv_grad = lax.psum_scatter(kv_grad.reshape(-1, 2 * kwidth), SEQ, scatter_dimension=0, tiled=True)
    tail_away, main = lax.optimization_barrier((tail_away, main))
    tail = (tail.astype(f32) + shift(tail_away, "core", 1).astype(f32)).astype(bf16)
    main = gather_all(sum_parts(main), SEQ)
    tail = exchange([tail[k] for k in range(SIDE)], "y").astype(bf16)
    tail, main = lax.optimization_barrier((tail, main))
    middle = main.shape[0] // 2
    ahead, behind = shift(main, "y", 1), shift(main, "y", -1)
    tokens_like = shape_of((micro, width, rows), bf16)
    input_grad, second_query_grad = simple(
        input_back_kernel,
        [VMEM] * 10,
        [tokens_like, tokens_like],
        (kv_grad, wk, wv, cosine, sine, normed_part, tokens, gain_one, middle_grad, second_query_grad),
        "input_back",
    )
    tail = scatter_sum(tail, SEQ)
    tail, ahead, behind = lax.optimization_barrier((tail, ahead, behind))
    tail = jnp.stack(collect(tail, "y"))
    places = SIDE * SIDE
    upper, lower = shift(ahead[:middle], "y", 1), shift(behind[middle:], "y", -1)
    tail, upper, lower = lax.optimization_barrier((tail, upper, lower))
    tail = lax.all_to_all(jnp.broadcast_to(tail[None], (places,) + tail.shape), SEQ, 0, 0)
    main = [main, ahead, upper, lower, behind]
    hidden = gate_weight.shape[1]
    main_away = [shift(v, "core", 1) for v in main]
    filled = unpack_main(main, width, hidden, None)
    gate, up, down = unpack_main(main_away, width, hidden, filled)
    tail, gate, up, down, input_grad, second_query_grad = lax.optimization_barrier(
        (tail, gate, up, down, input_grad, second_query_grad)
    )
    tail_away = shift(tail, "core", 1)
    square = shape_of((width, width), f32)
    narrow = shape_of((kwidth, width), f32)
    line = shape_of((width,), f32)
    q_total, k_total, v_total, o_total, gain_one_total, gain_two_total = pl.pallas_call(
        unpack_tail_kernel,
        in_specs=[VMEM] * 6,
        out_specs=[VMEM] * 6,
        out_shape=[square, narrow, narrow, square, line, line],
        scratch_shapes=[pltpu.VMEM((2 * math.prod(tail.shape[:3]), LANES), bf16)],
        compiler_params=params(),
        cost_estimate=cost(1),
        name="unpack_tail",
    )(tail, tail_away, query_weight, wk, wv, gain_one)
    return (
        jnp.swapaxes(result, 1, 2),
        jnp.swapaxes(input_grad, 1, 2),
        jnp.swapaxes(second_query_grad, 1, 2),
        gain_one_total,
        q_total,
        k_total.T,
        v_total.T,
        o_total,
        gain_two_total,
        gate,
        up,
        down.T,
    )


def exchange_all(value, axis):
    return [value.astype(f32)] + [shift(value, axis, k).astype(f32) for k in range(1, SIDE)]


def solution(mesh):
    grid = Mesh(mesh.devices.reshape(SIDE, SIDE, SIDE, 2), ("z", "x", "y", "core"))
    split = P(("y", "core"), SEQ, None)
    in_specs = (split, P(("y", "core"), None), split, split, split) + (P(),) * 9
    out_specs = (split, split, split) + (P(),) * 9
    return jax.shard_map(
        per_device, mesh=grid, in_specs=in_specs, out_specs=out_specs, check_vma=False
    )
```

```python
import functools
import math

import jax
import jax.numpy as jnp
from jax import lax
from jax.experimental import pallas as pl
from jax.experimental.pallas import tpu as pltpu
from jax.sharding import Mesh
from jax.sharding import PartitionSpec as P

HEADS = 9
KVH = 3
HD = 64
HALF = HD // 2
GROUP = HEADS // KVH
NEGATIVE = -1e30
EPSILON = 1e-05
ROPE_BASE = 100000.0
FACTOR = 1.0 / math.sqrt(HD)
LANES = 128
SIDE = 4
KEYS = 512
CHUNK = 256
SEQ = ("z", "x")
SIMPLE = {"kv_weights": 2.0, "input_back": 1.0, "prepare": 1.0, "query": 1.0}
f32 = jnp.float32
bf16 = jnp.bfloat16

VMEM = pl.BlockSpec(memory_space=pltpu.VMEM)
SMEM = pl.BlockSpec(memory_space=pltpu.SMEM)


def cost(microseconds):
    return pl.CostEstimate(flops=int(microseconds * 10**9), bytes_accessed=1000, transcendentals=0)


ANY = pl.BlockSpec(memory_space=pl.ANY)


def params(megabytes=56):
    return pltpu.CompilerParams(vmem_limit_bytes=megabytes * 1024 * 1024)


def shape_of(dims, dtype):
    return jax.ShapeDtypeStruct(dims, dtype)


def mul(left, right):
    return lax.dot_general(left, right, (((1,), (0,)), ((), ())), preferred_element_type=f32)


def mul_nt(left, right):
    return lax.dot_general(left, right, (((1,), (1,)), ((), ())), preferred_element_type=f32)


def flip(array):
    rows, cols = array.shape
    spare = -cols % LANES
    if spare:
        array = jnp.concatenate([array, jnp.zeros((rows, spare), array.dtype)], axis=1)
    extra = -rows % LANES
    if extra:
        array = jnp.concatenate([array, jnp.zeros((extra, cols + spare), array.dtype)], axis=0)
    return jnp.transpose(array)[:cols, :rows]


def side_by_side(ref):
    return jnp.concatenate([ref[m] for m in range(ref.shape[0])], axis=1)


def interleave(keys, values):
    parts = []
    for g in range(KVH):
        span = slice(g * HD, (g + 1) * HD)
        parts += [keys[span], values[span]]
    return jnp.concatenate(parts, axis=0)


def part_of(flat, index):
    return jnp.concatenate(
        [flat[(2 * g + index) * HD : (2 * g + index + 1) * HD] for g in range(KVH)], axis=0
    )


def own_block():
    return lax.axis_index("z") * SIDE + lax.axis_index("x")


def far_block():
    return SIDE * SIDE - 1 - own_block()


def turn(flat, cosine, sine, heads):
    parts = []
    for head in range(heads):
        front = flat[head * HD : head * HD + HALF]
        back = flat[head * HD + HALF : (head + 1) * HD]
        parts += [front * cosine - back * sine, back * cosine + front * sine]
    return parts


def simple(kernel, in_specs, outs, args, name):
    return pl.pallas_call(
        kernel,
        in_specs=in_specs,
        out_specs=[VMEM] * len(outs),
        out_shape=outs,
        compiler_params=params(),
        cost_estimate=cost(SIMPLE[name]),
        name=name,
    )(*args)


def prepare_kernel(lengths, tokens, gain, wk, wv, normed_out, kv_out, cos_out, sin_out, starts, far_starts):
    micro, _, rows = tokens.shape
    lane = lax.broadcasted_iota(jnp.int32, (1, rows), 1)
    places = own_block() * rows + lane
    far_places = far_block() * rows + lane
    positions = []
    for m in range(micro):
        start = jnp.zeros((1, rows), jnp.int32)
        far = jnp.zeros((1, rows), jnp.int32)
        end = jnp.int32(0)
        for j in range(lengths.shape[1]):
            length = lengths[m, j]
            end = end + length
            start = start + jnp.where(places >= end, length, 0)
            far = far + jnp.where(far_places >= end, length, 0)
        starts[m] = start
        far_starts[m] = far
        positions.append(places - start)
    order = lax.broadcasted_iota(jnp.int32, (HALF, micro * rows), 0).astype(f32)
    frequency = jnp.exp(order * (-2.0 * math.log(ROPE_BASE) / HD))
    angles = jnp.concatenate(positions, axis=1).astype(f32) * frequency
    cosine, sine = jnp.cos(angles), jnp.sin(angles)
    cos_out[...] = cosine
    sin_out[...] = sine
    inputs = side_by_side(tokens).astype(f32)
    scale = lax.rsqrt(jnp.mean(inputs * inputs, axis=0, keepdims=True) + EPSILON)
    line = gain[...].astype(f32).reshape(1, gain.shape[0])
    column = flip(jnp.broadcast_to(line, (LANES, gain.shape[0])))[:, :1]
    normed = (inputs * scale * column).astype(bf16)
    width = tokens.shape[1]
    for m in range(micro):
        span = slice(m * rows, (m + 1) * rows)
        normed_out[m, :width] = normed[:, span]
        base = width
        for table in (cosine, sine):
            high = table[:, span].astype(bf16)
            normed_out[m, base : base + HALF] = high
            normed_out[m, base + HALF : base + 2 * HALF] = (table[:, span] - high.astype(f32)).astype(bf16)
            base += 2 * HALF
    keys = turn(mul(wk[...], normed), cosine, sine, KVH)
    flat = interleave(jnp.concatenate(keys, axis=0), mul(wv[...], normed)).astype(bf16)
    for m in range(micro):
        kv_out[m] = flip(flat[:, m * rows : (m + 1) * rows])


def query_kernel(normed, weight, cos_ref, sin_ref, q1_out):
    width = weight.shape[0]
    flat = mul(flip(weight[...]), jnp.concatenate([normed[m, :width] for m in range(normed.shape[0])], axis=1))
    parts = turn(flat, cos_ref[...], sin_ref[...], HEADS)
    turned = (jnp.concatenate(parts, axis=0).astype(bf16) * FACTOR).astype(bf16)
    rows = q1_out.shape[2]
    for m in range(q1_out.shape[0]):
        q1_out[m] = turned[:, m * rows : (m + 1) * rows]


def lane_heads(ref, group):
    return jnp.concatenate(
        [ref[(group * GROUP + h) * HD : (group * GROUP + h + 1) * HD, :] for h in range(GROUP)], axis=1
    )


def visible_bias(start, block, first_key, rows):
    keys = first_key + lax.broadcasted_iota(jnp.int32, (KEYS, rows), 0)
    queries = block * rows + lax.broadcasted_iota(jnp.int32, (KEYS, rows), 1)
    seen = (keys >= start) & (keys <= queries)
    bias = jnp.where(seen, 0.0, NEGATIVE)
    return jnp.concatenate([bias] * GROUP, axis=1)


def key_steps(start, block, rows):
    per = KEYS // rows
    return jnp.min(start) // KEYS, block // per + 1


def run_forward(held, query, start, block_place, acc, peak, mass):
    rows = query.shape[1]
    per = KEYS // rows
    acc[...] = jnp.zeros_like(acc)
    peak[...] = jnp.full_like(peak, NEGATIVE)
    mass[...] = jnp.zeros_like(mass)
    first_step, last_step = key_steps(start, block_place, rows)

    @pl.loop(first_step, last_step)
    def _(step):
        block = held[pl.ds(step * per, per), 0].reshape(KEYS, held.shape[3])
        bias = visible_bias(start, block_place, step * KEYS, rows)
        tiles = [block[:, i * LANES : (i + 1) * LANES] for i in range(3)]
        for g in range(KVH):
            heads = lane_heads(query, g)
            scores = mul(tiles[g], jnp.concatenate([heads, jnp.zeros_like(heads)], axis=0)) + bias
            old = peak[g]
            top = jnp.maximum(old, jnp.max(scores, axis=0, keepdims=True))
            weights = jnp.exp(scores - top)
            decay = jnp.exp(old - top)
            values = jnp.transpose(tiles[g])[HD:]
            mass[g] = mass[g] * decay + jnp.sum(weights, axis=0, keepdims=True)
            acc[g] = acc[g] * decay + mul(values, weights.astype(bf16))
            peak[g] = top

    for g in range(KVH):
        acc[g] = acc[g] * (1.0 / mass[g])
        peak[g] = peak[g] + jnp.log(mass[g])


def forward_kernel(held, query_ref, starts, low_out, flat_out, lse_out, acc, peak, mass):
    query = query_ref.at[0]
    rows = query.shape[1]
    run_forward(held, query, starts[0], own_block(), acc, peak, mass)
    for g in range(KVH):
        lse_out[0, g] = peak[g]
        for h in range(GROUP):
            head = g * GROUP + h
            flat_out[0, head * HD : (head + 1) * HD, :] = acc[g, :, h * rows : (h + 1) * rows]
    low_out[...] = flat_out[...].astype(bf16)


def one_of(dims, axis=0):
    block = tuple(1 if i == axis else n for i, n in enumerate(dims))
    return pl.BlockSpec(block, lambda m: tuple(m if i == axis else 0 for i in range(len(dims))))


def attend_forward(kv, query, starts):
    micro, width, rows = query.shape
    lanes = GROUP * rows
    low = shape_of(query.shape, bf16)
    flat = shape_of(query.shape, f32)
    lse = shape_of((micro, KVH, 1, lanes), f32)
    return pl.pallas_call(
        forward_kernel,
        grid=(micro,),
        in_specs=[one_of(kv.shape, 1), one_of(query.shape), one_of(starts.shape)],
        out_specs=[one_of(v.shape) for v in (low, flat, lse)],
        out_shape=[low, flat, lse],
        scratch_shapes=[
            pltpu.VMEM((KVH, HD, lanes), f32),
            pltpu.VMEM((KVH, 1, lanes), f32),
            pltpu.VMEM((KVH, 1, lanes), f32),
        ],
        compiler_params=params(),
        cost_estimate=cost(2.5),
        name="attention_forward",
    )(kv, query, starts)


def backward_kernel(
    held, q1_ref, q2_ref, d1_ref, d2_ref, o1, lse1, starts, far_starts, cos_ref, sin_ref,
    kv_out, first_grad, second_grad, sums, delta, dq, query2, both, acc, peak, mass,
):
    rows = q1_ref.shape[2]
    per = KEYS // rows
    query2[...] = (q2_ref[0] * FACTOR).astype(bf16)
    sums[...] = jnp.zeros_like(sums)
    dq[...] = jnp.zeros_like(dq)

    def attention(a, q_ref, d_ref, outs, lse, start, block_place):
        for g in range(KVH):
            query, grad = lane_heads(q_ref, g), lane_heads(d_ref, g)
            delta[a, g] = jnp.sum(grad.astype(f32) * outs(g), axis=0, keepdims=True)
            zero = jnp.zeros_like(query)
            both[g] = jnp.concatenate(
                [jnp.concatenate([query, zero], axis=1), jnp.concatenate([zero, grad], axis=1)], axis=0
            )
        first_step, last_step = key_steps(start, block_place, rows)

        @pl.loop(first_step, last_step)
        def _(step):
            block = held[pl.ds(step * per, per), 0].reshape(KEYS, held.shape[3])
            bias = visible_bias(start, block_place, step * KEYS, rows)
            tiles = [block[:, i * LANES : (i + 1) * LANES] for i in range(3)]
            total = []
            for g in range(KVH):
                pair = both[g]
                lanes = pair.shape[1] // 2
                products = mul(tiles[g], pair)
                weights = jnp.exp(products[:, :lanes] + bias - lse[g])
                score_grad = (weights * (products[:, lanes:] - delta[a, g])).astype(bf16)
                dq[a, g] += mul(jnp.transpose(tiles[g])[:HD], score_grad)
                total.append(mul_nt(jnp.concatenate([score_grad, weights.astype(bf16)], axis=1), pair))
            joined = jnp.concatenate(total, axis=1)
            sums[pl.ds(step * per, per)] += joined.reshape(per, rows, joined.shape[1])

    run_forward(held, query2, far_starts[0], far_block(), acc, peak, mass)
    attention(0, q1_ref.at[0], d1_ref.at[0], lambda g: lane_heads(o1.at[0], g), lse1.at[0], starts[0], own_block())
    attention(1, query2, d2_ref.at[0], lambda g: acc[g], peak, far_starts[0], far_block())
    kv_out[:, 0] = sums[...].astype(bf16)
    cosine, sine = cos_ref[...], -sin_ref[...]
    for g in range(KVH):
        for h in range(GROUP):
            head = g * GROUP + h
            lanes = slice(h * rows, (h + 1) * rows)
            target = slice(head * HD, (head + 1) * HD)
            parts = turn(dq[0, g][:, lanes] * FACTOR, cosine, sine, 1)
            first_grad[0, target, :] = jnp.concatenate(parts, axis=0).astype(bf16)
            second_grad[0, target, :] = (dq[1, g][:, lanes] * FACTOR).astype(bf16)


def attend_backward(kv, *arrays):
    micro, width, rows = arrays[0].shape
    lanes = GROUP * rows
    blocks, _, _, kv_width = kv.shape
    part = shape_of((micro, width, rows), bf16)
    table = pl.BlockSpec((HALF, rows), lambda m: (0, m))
    return pl.pallas_call(
        backward_kernel,
        grid=(micro,),
        in_specs=[one_of(kv.shape, 1)] + [one_of(v.shape) for v in arrays[:-2]] + [table] * 2,
        out_specs=[one_of(kv.shape, 1)] + [one_of(part.shape)] * 2,
        out_shape=[shape_of(kv.shape, bf16), part, part],
        scratch_shapes=[
            pltpu.VMEM((blocks, rows, kv_width), f32),
            pltpu.VMEM((2, KVH, 1, lanes), f32),
            pltpu.VMEM((2, KVH, HD, lanes), f32),
            pltpu.VMEM((width, rows), bf16),
            pltpu.VMEM((KVH, 2 * HD, 2 * lanes), bf16),
            pltpu.VMEM((KVH, HD, lanes), f32),
            pltpu.VMEM((KVH, 1, lanes), f32),
            pltpu.VMEM((KVH, 1, lanes), f32),
        ],
        compiler_params=params(),
        cost_estimate=cost(7),
        name="attention_backward",
    )(kv, *arrays)


def weights_kernel(
    sums, normed, starts, far_starts, own_normed, grad_ref, weight, wo_grad, gain_two_grad,
    normed_grad, kept, away, kv_out, packed,
):
    rows = starts.shape[2]
    width = weight.shape[0]
    per = KEYS // rows

    @pl.when(pl.program_id(0) == 0)
    def _():
        kv_out[...] = jnp.zeros_like(kv_out)

    def add(step):
        block = sums[pl.ds(step * per, per), 0].reshape(KEYS, sums.shape[3])
        inner = [normed[step * per + i, 0] for i in range(per)]
        values = jnp.concatenate([v[:width] for v in inner], axis=1)
        tables = jnp.concatenate([v[width:] for v in inner], axis=1).astype(f32)
        cosine = tables[:HALF] + tables[HALF : 2 * HALF]
        sine = tables[2 * HALF : 3 * HALF] + tables[3 * HALF :]
        flat = jnp.concatenate([jnp.transpose(block[:, g * LANES : (g + 1) * LANES]) for g in range(KVH)], axis=0)
        keys = turn(part_of(flat, 0).astype(f32), cosine, -sine, KVH)
        both = jnp.concatenate([jnp.concatenate(keys, axis=0).astype(bf16), part_of(flat, 1)], axis=0)
        kv_out[...] += mul_nt(both, values)

    near = key_steps(starts[0], own_block(), rows)
    far = key_steps(far_starts[0], far_block(), rows)
    pl.loop(*near)(add)

    @pl.loop(*far)
    def _(step):
        pl.when((step < near[0]) | (step >= near[1]))(lambda: add(step))


    @pl.when(pl.program_id(0) == pl.num_programs(0) - 1)
    def _():
        grad = side_by_side(grad_ref)
        values = jnp.concatenate([own_normed[m, :width] for m in range(own_normed.shape[0])], axis=1)
        normed_grad[...] = mul(weight[...], grad)
        lane = lax.broadcasted_iota(jnp.int32, (width, LANES), 1)
        gains = flip(jnp.where(lane == 0, gain_two_grad[...], 0.0))[:16]
        base = 0
        for array in (mul_nt(values, grad), kv_out[...], wo_grad[...], gains):
            base = pack_rows(packed, base, array.astype(bf16))
        packed[base:] = jnp.zeros((packed.shape[0] - base, LANES), bf16)
        unit = kept.shape[1]
        for dy in range(SIDE):
            for target, dc in ((kept, 0), (away, 1)):
                target[dy] = packed[pl.ds(pl.multiple_of(place_of(dc, dy, 1) * unit, 16), unit)]


def weights_back(sums, normed, starts, far_starts, *others):
    micro, _, rows = starts.shape
    width = others[2].shape[0]
    kv_width = sums.shape[3]
    unit = tail_rows(width)
    tail = shape_of((SIDE, unit, LANES), bf16)
    outs = [shape_of((width, micro * rows), f32), tail, tail]

    def whole(v):
        return pl.BlockSpec(v.shape, lambda m: (0,) * len(v.shape))

    return pl.pallas_call(
        weights_kernel,
        grid=(micro,),
        in_specs=[one_of(sums.shape, 1), one_of(normed.shape, 1), one_of(starts.shape), one_of(starts.shape)]
        + [whole(v) for v in others],
        out_specs=[whole(v) for v in outs],
        out_shape=outs,
        scratch_shapes=[
            pltpu.VMEM((kv_width, width), f32),
            pltpu.VMEM((2 * SIDE * unit, LANES), bf16),
        ],
        compiler_params=params(),
        cost_estimate=cost(3),
        name="weights_back",
    )(sums, normed, starts, far_starts, *others)


def norm_back(vector, scale, gain, gradient):
    weighted = gradient * gain
    gain_grad = jnp.sum(gradient * vector * scale, axis=1, keepdims=True)
    inner = jnp.mean(weighted * vector, axis=0, keepdims=True)
    return scale * weighted - vector * (scale * scale * scale * inner), gain_grad


def ffn_kernel(
    last, core, first, tokens, out_weight, gain, out_grad, wg, wu, wd, *refs,
):
    step = pl.program_id(0)
    micro, width, rows = tokens.shape
    if last:
        before, result_before, grad_before = refs[:3]
        result, main, middle_grad, d1, gain_grad, wo_grad = refs[3:9]
        normed, normed_t, grad, grad_t, result_sum, normed_grad = refs[9:]
        middle = before
    else:
        main, middle, result_sum, normed_grad = refs[:4]
        normed, normed_t, grad, grad_t = refs[4:]

    @pl.when(step == 0)
    def _():
        if last:
            value = before[...]
            result_sum[...] = result_before[...]
            normed_grad[...] = grad_before[...]
        else:
            value = side_by_side(tokens).astype(f32) + mul(flip(out_weight[...]), side_by_side(first))
            middle[...] = value
            result_sum[...] = jnp.zeros_like(result_sum)
            normed_grad[...] = jnp.zeros_like(normed_grad)
        scale = lax.rsqrt(jnp.mean(value * value, axis=0, keepdims=True) + EPSILON)
        low = (value * scale * gain[...].astype(f32)).astype(bf16)
        normed_t[...] = low
        normed[...] = flip(low)
        flat = side_by_side(out_grad)
        grad_t[...] = flat
        grad[...] = flip(flat)

    low = normed[...]
    gate = mul(low, wg[...])
    up = mul(low, wu[...])
    sigmoid = 1.0 / (1.0 + jnp.exp(-gate))
    active = gate * sigmoid
    hidden = (active * up).astype(bf16)
    result_sum[...] += mul_nt(hidden, wd[...])
    hidden_grad = mul(grad[...], wd[...])
    gate_grad = (hidden_grad * up * sigmoid * (1.0 + gate * (1.0 - sigmoid))).astype(bf16)
    up_grad = (hidden_grad * active).astype(bf16)
    parts = (mul(normed_t[...], gate_grad), mul(normed_t[...], up_grad), mul(grad_t[...], hidden))
    for i in range(CHUNK // LANES):
        span = slice(i * LANES, (i + 1) * LANES)
        for k, part in enumerate(parts):
            rows_at = slice((i * 3 + k) * width, (i * 3 + k + 1) * width)
            main[rows_at] = part[:, span].astype(bf16)
    normed_grad[...] += mul_nt(gate_grad, wg[...]) + mul_nt(up_grad, wu[...])
    if not last:
        return

    @pl.when(step == pl.num_programs(0) - 1)
    def _():
        value = middle[...]
        final = (value + flip(result_sum[...])).astype(bf16)
        scale = lax.rsqrt(jnp.mean(value * value, axis=0, keepdims=True) + EPSILON)
        part, gains = norm_back(value, scale, gain[...].astype(f32), flip(normed_grad[...]))
        gain_grad[...] = gains
        total = grad_t[...].astype(f32) + part
        middle_grad[...] = total
        branch = total.astype(bf16)
        wo_grad[...] = mul_nt(side_by_side(first), branch).astype(bf16)
        back = mul(out_weight[...], branch).astype(bf16)
        for m in range(micro):
            span = slice(m * rows, (m + 1) * rows)
            d1[m] = back[:, span]
            result[m] = final[:, span]


def pack_rows(target, base, array):
    rows, cols = array.shape
    for i in range(-(-cols // LANES)):
        span = array[:, i * LANES : (i + 1) * LANES]
        if span.shape[1] < LANES:
            span = jnp.concatenate([span, jnp.zeros((rows, LANES - span.shape[1]), span.dtype)], axis=1)
        target[base : base + rows] = span
        base += rows
    return base


def main_rows(width, hidden):
    used = hidden // 2 // LANES * 3 * width
    unit = SIDE * SIDE * SIDE * 8
    return -(-used // unit) * unit


def feed_forward(core, first, tokens, out_weight, gain, out_grad, wg, wu, wd, before):
    micro, width, rows = tokens.shape
    total = micro * rows
    hidden = wg.shape[1]
    steps = hidden // 2 // CHUNK
    block = pl.BlockSpec((CHUNK // LANES * 3 * width, LANES), lambda i, c: (i, 0))
    last = len(before) > 0

    def whole(*dims):
        return pl.BlockSpec(dims, lambda i, c: (0,) * len(dims))

    def column(i, c):
        side = c[0] if last else 1 - c[0]
        return (0, side * steps + i)

    weight = pl.BlockSpec((width, CHUNK), column)
    flat, natural = shape_of((width, total), f32), shape_of((total, width), f32)
    spec, tall = whole(width, total), whole(total, width)
    token_spec, token_shape = whole(micro, width, rows), shape_of((micro, width, rows), bf16)
    if last:
        outs = [
            (token_shape, token_spec),
            (shape_of((main_rows(width, hidden), LANES), bf16), block),
            (flat, spec),
            (token_shape, token_spec),
            (shape_of((width, 1), f32), whole(width, 1)),
            (shape_of((width, width), bf16), whole(width, width)),
        ]
        more = [spec, tall, tall]
        scratch = [pltpu.VMEM((total, width), f32)] * 2
    else:
        outs = [
            (shape_of((main_rows(width, hidden), LANES), bf16), block),
            (flat, spec),
            (natural, tall),
            (natural, tall),
        ]
        more, scratch = [], []
    low = [pltpu.VMEM((total, width), bf16), pltpu.VMEM((width, total), bf16)]
    return pl.pallas_call(
        functools.partial(ffn_kernel, last),
        grid_spec=pltpu.PrefetchScalarGridSpec(
            num_scalar_prefetch=1,
            grid=(steps,),
            in_specs=[
                token_spec,
                token_spec,
                whole(width, width),
                whole(width, 1),
                token_spec,
                weight,
                weight,
                weight,
            ]
            + more,
            out_specs=[v[1] for v in outs],
            scratch_shapes=low * 2 + scratch,
        ),
        out_shape=[v[0] for v in outs],
        compiler_params=params(),
        cost_estimate=cost(3),
        name="feed_forward",
    )(core, first, tokens, out_weight, gain, out_grad, wg, wu, wd, *before)


def tail_rows(width):
    tiles = -(-width // LANES)
    used = tiles * (2 * width + 2 * KVH * HD + 16)
    unit = 2 * SIDE * SIDE * SIDE * 8
    return -(-used // unit) * (unit // 2 // SIDE)


def place_of(dc, dy, sign):
    cc = lax.rem(lax.axis_index("core") + dc, 2)
    yy = lax.rem(lax.axis_index("y") + sign * dy + SIDE, SIDE)
    return cc * SIDE + yy


def input_back_kernel(
    kv_grad, wk, wv, cos_ref, sin_ref, partial, tokens, gain, middle_grad, second, input_grad, second_grad
):
    second_grad[...] = second[...]
    micro, width, rows = tokens.shape
    flat = jnp.concatenate(
        [flip(kv_grad[m * rows : (m + 1) * rows].astype(f32)) for m in range(micro)], axis=1
    )
    parts = turn(part_of(flat, 0), cos_ref[...], -sin_ref[...], KVH)
    low = jnp.concatenate(parts + [part_of(flat, 1)], axis=0).astype(bf16)
    weights = flip(jnp.concatenate([wk[...], wv[...]], axis=0))
    normed_grad = partial[...] + mul(weights, low)
    inputs = side_by_side(tokens).astype(f32)
    scale = lax.rsqrt(jnp.mean(inputs * inputs, axis=0, keepdims=True) + EPSILON)
    part, _ = norm_back(inputs, scale, gain[...].astype(f32), normed_grad)
    final = (middle_grad[...] + part).astype(bf16)
    for m in range(micro):
        input_grad[m] = final[:, m * rows : (m + 1) * rows]


def unpack_tail_kernel(kept, away, wq, wk, wv, gain, q_out, k_out, v_out, o_out, gain_one, gain_two, held):
    places, _, rows, _ = kept.shape
    for dy in range(SIDE):
        for source, dc in ((kept, 0), (away, 1)):
            base = place_of(dc, dy, -1) * places * rows
            for i in range(places):
                held[pl.ds(pl.multiple_of(base + i * rows, 16), rows)] = source[i, dy]
    width = q_out.shape[0]
    cut = k_out.shape[0]
    base = 0

    def section(rows, cols):
        nonlocal base
        count = -(-cols // LANES)
        parts = [held[base + i * rows : base + (i + 1) * rows] for i in range(count)]
        base += count * rows
        return jnp.concatenate(parts, axis=1)[:, :cols].astype(f32)

    query = section(width, width)
    both = section(2 * cut, width)
    key, value = both[:cut], both[cut:]
    q_out[...] = query
    k_out[...] = key
    v_out[...] = value
    o_out[...] = section(width, width)
    gain_two[...] = section(16, width)[0]
    total = jnp.sum(query * wq[...].astype(f32), axis=1, keepdims=True) / gain[...].astype(f32)
    total = flip(jnp.broadcast_to(total, (width, LANES)))[0:1]
    rest = jnp.sum(key * wk[...].astype(f32), axis=0, keepdims=True)
    rest = rest + jnp.sum(value * wv[...].astype(f32), axis=0, keepdims=True)
    line = flip(jnp.broadcast_to(gain[...].astype(f32), (width, LANES)))[0:1]
    gain_one[...] = (total + rest / line)[0]


def unpack_main_kernel(other, *refs):
    pieces = refs[: SIDE + 1]
    gate, up, down, held, wide, sems = refs[-6:]
    unit = pieces[0].shape[0]
    half = unit // 2
    for k, offset, piece in zip((0, 1, 2, 2, 3), (0, 0, 0, half, 0), pieces):
        place = lax.rem(lax.axis_index("y") - k + SIDE, SIDE)
        held[pl.ds(pl.multiple_of(place * unit + offset, 16), piece.shape[0])] = piece[...]
    core = lax.axis_index("core")
    core = 1 - core if other else core
    width, cols = wide.shape[1:]
    copies = []
    for k, target in enumerate((gate, up, down)):
        for t in range(cols // LANES):
            base = (t * 3 + k) * width
            wide[k, :, t * LANES : (t + 1) * LANES] = held[base : base + width].astype(f32)
        span = pl.ds(pl.multiple_of(core * cols, LANES), cols)
        copies.append(pltpu.make_async_copy(wide.at[k], target.at[:, span], sems.at[k]))
        copies[-1].start()
    for copy in copies:
        copy.wait()


def unpack_main(pieces, width, hidden, filled):
    unit = pieces[0].shape[0]
    outs = [shape_of((width, hidden), f32)] * 3
    return pl.pallas_call(
        functools.partial(unpack_main_kernel, filled is not None),
        in_specs=[VMEM] * len(pieces) + ([ANY] * 3 if filled else []),
        out_specs=[ANY] * 3,
        out_shape=outs,
        scratch_shapes=[
            pltpu.VMEM((SIDE * unit, LANES), bf16),
            pltpu.VMEM((3, width, hidden // 2), f32),
            pltpu.SemaphoreType.DMA((3,)),
        ],
        input_output_aliases={len(pieces) + i: i for i in range(3)} if filled else {},
        compiler_params=params(),
        cost_estimate=cost(1.5),
        name="unpack_main",
    )(*pieces, *(filled or ()))


def shift(value, axis, distance):
    size = lax.axis_size(axis)
    return lax.ppermute(value, axis, [(i, (i + distance) % size) for i in range(size)])


def mirror(value):
    size = SIDE * SIDE
    return lax.ppermute(value, SEQ, [(i, size - 1 - i) for i in range(size)])


def collect(value, axis):
    return [value] + [shift(value, axis, k) for k in range(1, SIDE)]


def exchange(parts, axis):
    total = parts[0].astype(f32)
    for k in range(1, SIDE):
        total = total + shift(parts[k], axis, k).astype(f32)
    return total


def scatter_parts(held, axis):
    rows, lanes = held.shape
    places = lax.axis_size(axis)
    return lax.all_to_all(held.reshape(places, rows // places, lanes), axis, 0, 0)


def sum_parts(parts):
    return jnp.sum(parts.astype(f32), axis=0).astype(bf16)


def scatter_sum(held, axis):
    return sum_parts(scatter_parts(held, axis))


def gather_all(held, axis):
    rows, lanes = held.shape
    places = lax.axis_size(axis)
    spread = jnp.broadcast_to(held[None], (places,) + held.shape)
    return lax.all_to_all(spread, axis, 0, 0).reshape(places * rows, lanes)


def after(value, *others):
    return lax.optimization_barrier((value, *others))[0]


def per_device(
    tokens,
    doc_lengths,
    second_query,
    second_grad,
    out_grad,
    first_gain,
    query_weight,
    key_weight,
    value_weight,
    output_weight,
    second_gain,
    gate_weight,
    up_weight,
    down_weight,
):
    micro, rows, width = tokens.shape
    kwidth = key_weight.shape[1]
    total = micro * rows
    tiles = -(-width // LANES)
    core = lax.axis_index("core").reshape(1)
    tokens, second_query, second_grad, out_grad = (
        jnp.swapaxes(v, 1, 2) for v in (tokens, second_query, second_grad, out_grad)
    )
    wk, wv, wd = key_weight.T, value_weight.T, down_weight.T
    gain_one, gain_two = first_gain.reshape(width, 1), second_gain.reshape(width, 1)

    table = shape_of((HALF, total), f32)
    start = shape_of((micro, 1, rows), jnp.int32)
    normed, kv, cosine, sine, starts, far_starts = simple(
        prepare_kernel,
        [SMEM] + [VMEM] * 4,
        [
            shape_of((micro, width + 4 * HALF, rows), bf16),
            shape_of((micro, rows, 2 * kwidth), bf16),
            table,
            table,
            start,
            start,
        ],
        (doc_lengths, tokens, first_gain, wk, wv),
        "prepare",
    )
    kv = lax.all_gather(kv, SEQ, axis=0)
    (q1,) = simple(
        query_kernel,
        [VMEM] * 4,
        [shape_of((micro, width, rows), bf16)],
        (normed, query_weight, cosine, sine),
        "query",
    )
    far_query, far_grad = mirror(second_query), mirror(second_grad)
    kv, q1, far_query, far_grad, gathered = lax.optimization_barrier((kv, q1, far_query, far_grad, normed))
    gathered = lax.all_gather(gathered, SEQ, axis=0)
    first_low, first_flat, first_lse = attend_forward(kv, q1, starts)
    ffn_args = (first_low, tokens, output_weight, gain_two, out_grad, gate_weight, up_weight, wd)
    away, *before = feed_forward(core, *ffn_args, ())
    result, main, middle_grad, d1, gain_two_grad, wo_grad = feed_forward(core, *ffn_args, before)
    main = (main.astype(f32) + shift(away, "core", 1).astype(f32)).astype(bf16)
    main = scatter_parts(main, "y")
    kv_grad, query_grad, second_query_grad = attend_backward(
        kv,
        q1,
        far_query,
        d1,
        far_grad,
        first_flat,
        first_lse,
        starts,
        far_starts,
        cosine,
        sine,
    )
    second_query_grad = mirror(second_query_grad)
    kv_grad, gathered, main = lax.optimization_barrier((kv_grad, gathered, main))
    main = scatter_parts(sum_parts(main), SEQ)
    normed_part, tail, tail_away = weights_back(
        kv_grad, gathered, starts, far_starts, normed, query_grad, query_weight, wo_grad, gain_two_grad
    )
    kv_grad = lax.psum_scatter(kv_grad.reshape(-1, 2 * kwidth), SEQ, scatter_dimension=0, tiled=True)
    tail_away, main = lax.optimization_barrier((tail_away, main))
    tail = (tail.astype(f32) + shift(tail_away, "core", 1).astype(f32)).astype(bf16)
    main = gather_all(sum_parts(main), SEQ)
    tail = exchange([tail[k] for k in range(SIDE)], "y").astype(bf16)
    tail, main, second_query_grad = lax.optimization_barrier((tail, main, second_query_grad))
    middle = main.shape[0] // 2
    ahead, behind = shift(main, "y", 1), shift(main, "y", -1)
    tokens_like = shape_of((micro, width, rows), bf16)
    input_grad, second_query_grad = simple(
        input_back_kernel,
        [VMEM] * 10,
        [tokens_like, tokens_like],
        (kv_grad, wk, wv, cosine, sine, normed_part, tokens, gain_one, middle_grad, second_query_grad),
        "input_back",
    )
    tail = scatter_sum(tail, SEQ)
    tail, ahead, behind = lax.optimization_barrier((tail, ahead, behind))
    tail = jnp.stack(collect(tail, "y"))
    places = SIDE * SIDE
    upper, lower = shift(ahead[:middle], "y", 1), shift(behind[middle:], "y", -1)
    tail, upper, lower = lax.optimization_barrier((tail, upper, lower))
    tail = lax.all_to_all(jnp.broadcast_to(tail[None], (places,) + tail.shape), SEQ, 0, 0)
    main = [main, ahead, upper, lower, behind]
    hidden = gate_weight.shape[1]
    main_away = [shift(v, "core", 1) for v in main]
    filled = unpack_main(main, width, hidden, None)
    gate, up, down = unpack_main(main_away, width, hidden, filled)
    tail, gate, up, down, input_grad, second_query_grad = lax.optimization_barrier(
        (tail, gate, up, down, input_grad, second_query_grad)
    )
    tail_away = shift(tail, "core", 1)
    square = shape_of((width, width), f32)
    narrow = shape_of((kwidth, width), f32)
    line = shape_of((width,), f32)
    q_total, k_total, v_total, o_total, gain_one_total, gain_two_total = pl.pallas_call(
        unpack_tail_kernel,
        in_specs=[VMEM] * 6,
        out_specs=[VMEM] * 6,
        out_shape=[square, narrow, narrow, square, line, line],
        scratch_shapes=[pltpu.VMEM((2 * math.prod(tail.shape[:3]), LANES), bf16)],
        compiler_params=params(),
        cost_estimate=cost(1),
        name="unpack_tail",
    )(tail, tail_away, query_weight, wk, wv, gain_one)
    return (
        jnp.swapaxes(result, 1, 2),
        jnp.swapaxes(input_grad, 1, 2),
        jnp.swapaxes(second_query_grad, 1, 2),
        gain_one_total,
        q_total,
        k_total.T,
        v_total.T,
        o_total,
        gain_two_total,
        gate,
        up,
        down.T,
    )


def exchange_all(value, axis):
    return [value.astype(f32)] + [shift(value, axis, k).astype(f32) for k in range(1, SIDE)]


def solution(mesh):
    grid = Mesh(mesh.devices.reshape(SIDE, SIDE, SIDE, 2), ("z", "x", "y", "core"))
    split = P(("y", "core"), SEQ, None)
    in_specs = (split, P(("y", "core"), None), split, split, split) + (P(),) * 9
    out_specs = (split, split, split) + (P(),) * 9
    return jax.shard_map(
        per_device, mesh=grid, in_specs=in_specs, out_specs=out_specs, check_vma=False
    )
```

```python
import functools
import math

import jax
import jax.numpy as jnp
from jax import lax
from jax.experimental import pallas as pl
from jax.experimental.pallas import tpu as pltpu
from jax.sharding import Mesh
from jax.sharding import PartitionSpec as P

HEADS = 9
KVH = 3
HD = 64
HALF = HD // 2
GROUP = HEADS // KVH
NEGATIVE = -1e30
EPSILON = 1e-05
ROPE_BASE = 100000.0
FACTOR = 1.0 / math.sqrt(HD)
LANES = 128
SIDE = 4
KEYS = 512
CHUNK = 256
SEQ = ("z", "x")
SIMPLE = {"kv_weights": 2.0, "input_back": 1.0, "prepare": 1.0, "query": 1.0}
f32 = jnp.float32
bf16 = jnp.bfloat16

VMEM = pl.BlockSpec(memory_space=pltpu.VMEM)
SMEM = pl.BlockSpec(memory_space=pltpu.SMEM)


def cost(microseconds):
    return pl.CostEstimate(flops=int(microseconds * 10**9), bytes_accessed=1000, transcendentals=0)


ANY = pl.BlockSpec(memory_space=pl.ANY)


def params(megabytes=56):
    return pltpu.CompilerParams(vmem_limit_bytes=megabytes * 1024 * 1024)


def shape_of(dims, dtype):
    return jax.ShapeDtypeStruct(dims, dtype)


def mul(left, right):
    return lax.dot_general(left, right, (((1,), (0,)), ((), ())), preferred_element_type=f32)


def mul_nt(left, right):
    return lax.dot_general(left, right, (((1,), (1,)), ((), ())), preferred_element_type=f32)


def flip(array):
    rows, cols = array.shape
    spare = -cols % LANES
    if spare:
        array = jnp.concatenate([array, jnp.zeros((rows, spare), array.dtype)], axis=1)
    extra = -rows % LANES
    if extra:
        array = jnp.concatenate([array, jnp.zeros((extra, cols + spare), array.dtype)], axis=0)
    return jnp.transpose(array)[:cols, :rows]


def side_by_side(ref):
    return jnp.concatenate([ref[m] for m in range(ref.shape[0])], axis=1)


def interleave(keys, values):
    parts = []
    for g in range(KVH):
        span = slice(g * HD, (g + 1) * HD)
        parts += [keys[span], values[span]]
    return jnp.concatenate(parts, axis=0)


def part_of(flat, index):
    return jnp.concatenate(
        [flat[(2 * g + index) * HD : (2 * g + index + 1) * HD] for g in range(KVH)], axis=0
    )


def own_block():
    return lax.axis_index("z") * SIDE + lax.axis_index("x")


def far_block():
    return SIDE * SIDE - 1 - own_block()


def turn(flat, cosine, sine, heads):
    parts = []
    for head in range(heads):
        front = flat[head * HD : head * HD + HALF]
        back = flat[head * HD + HALF : (head + 1) * HD]
        parts += [front * cosine - back * sine, back * cosine + front * sine]
    return parts


def simple(kernel, in_specs, outs, args, name):
    return pl.pallas_call(
        kernel,
        in_specs=in_specs,
        out_specs=[VMEM] * len(outs),
        out_shape=outs,
        compiler_params=params(),
        cost_estimate=cost(SIMPLE[name]),
        name=name,
    )(*args)


def prepare_kernel(lengths, tokens, gain, wk, wv, normed_out, kv_out, cos_out, sin_out, starts, far_starts):
    micro, _, rows = tokens.shape
    lane = lax.broadcasted_iota(jnp.int32, (1, rows), 1)
    places = own_block() * rows + lane
    far_places = far_block() * rows + lane
    positions = []
    for m in range(micro):
        start = jnp.zeros((1, rows), jnp.int32)
        far = jnp.zeros((1, rows), jnp.int32)
        end = jnp.int32(0)
        for j in range(lengths.shape[1]):
            length = lengths[m, j]
            end = end + length
            start = start + jnp.where(places >= end, length, 0)
            far = far + jnp.where(far_places >= end, length, 0)
        starts[m] = start
        far_starts[m] = far
        positions.append(places - start)
    order = lax.broadcasted_iota(jnp.int32, (HALF, micro * rows), 0).astype(f32)
    frequency = jnp.exp(order * (-2.0 * math.log(ROPE_BASE) / HD))
    angles = jnp.concatenate(positions, axis=1).astype(f32) * frequency
    cosine, sine = jnp.cos(angles), jnp.sin(angles)
    cos_out[...] = cosine
    sin_out[...] = sine
    inputs = side_by_side(tokens).astype(f32)
    scale = lax.rsqrt(jnp.mean(inputs * inputs, axis=0, keepdims=True) + EPSILON)
    line = gain[...].astype(f32).reshape(1, gain.shape[0])
    column = flip(jnp.broadcast_to(line, (LANES, gain.shape[0])))[:, :1]
    normed = (inputs * scale * column).astype(bf16)
    width = tokens.shape[1]
    for m in range(micro):
        span = slice(m * rows, (m + 1) * rows)
        normed_out[m, :width] = normed[:, span]
        base = width
        for table in (cosine, sine):
            high = table[:, span].astype(bf16)
            normed_out[m, base : base + HALF] = high
            normed_out[m, base + HALF : base + 2 * HALF] = (table[:, span] - high.astype(f32)).astype(bf16)
            base += 2 * HALF
    keys = turn(mul(wk[...], normed), cosine, sine, KVH)
    flat = interleave(jnp.concatenate(keys, axis=0), mul(wv[...], normed)).astype(bf16)
    for m in range(micro):
        kv_out[m] = flip(flat[:, m * rows : (m + 1) * rows])


def query_kernel(normed, weight, cos_ref, sin_ref, q1_out):
    width = weight.shape[0]
    flat = mul(flip(weight[...]), jnp.concatenate([normed[m, :width] for m in range(normed.shape[0])], axis=1))
    parts = turn(flat, cos_ref[...], sin_ref[...], HEADS)
    turned = (jnp.concatenate(parts, axis=0).astype(bf16) * FACTOR).astype(bf16)
    rows = q1_out.shape[2]
    for m in range(q1_out.shape[0]):
        q1_out[m] = turned[:, m * rows : (m + 1) * rows]


def lane_heads(ref, group):
    return jnp.concatenate(
        [ref[(group * GROUP + h) * HD : (group * GROUP + h + 1) * HD, :] for h in range(GROUP)], axis=1
    )


def visible_bias(start, block, first_key, limit, rows):
    keys = first_key + lax.broadcasted_iota(jnp.int32, (KEYS, rows), 0)
    queries = block * rows + lax.broadcasted_iota(jnp.int32, (KEYS, rows), 1)
    seen = (keys >= start) & (keys <= queries) & (keys < limit)
    bias = jnp.where(seen, 0.0, NEGATIVE)
    return jnp.concatenate([bias] * GROUP, axis=1)


def key_steps(start, block, rows):
    per = KEYS // rows
    return jnp.min(start) // KEYS, block // per + 1


def key_windows(start, block, rows):
    per = KEYS // rows
    return (block - jnp.min(start) // rows + per) // per


def window(held, step, start, block, rows):
    per = KEYS // rows
    end = block + 1 - step * per
    first = jnp.maximum(end - per, 0)
    keys = held[pl.ds(first, per), 0].reshape(KEYS, held.shape[3])
    return first, keys, visible_bias(start, block, first * rows, end * rows, rows)


def run_forward(held, query, start, block_place, acc, peak, mass):
    rows = query.shape[1]
    acc[...] = jnp.zeros_like(acc)
    peak[...] = jnp.full_like(peak, NEGATIVE)
    mass[...] = jnp.zeros_like(mass)

    @pl.loop(0, key_windows(start, block_place, rows))
    def _(step):
        _, block, bias = window(held, step, start, block_place, rows)
        tiles = [block[:, i * LANES : (i + 1) * LANES] for i in range(3)]
        for g in range(KVH):
            heads = lane_heads(query, g)
            scores = mul(tiles[g], jnp.concatenate([heads, jnp.zeros_like(heads)], axis=0)) + bias
            old = peak[g]
            top = jnp.maximum(old, jnp.max(scores, axis=0, keepdims=True))
            weights = jnp.exp(scores - top)
            decay = jnp.exp(old - top)
            values = jnp.transpose(tiles[g])[HD:]
            mass[g] = mass[g] * decay + jnp.sum(weights, axis=0, keepdims=True)
            acc[g] = acc[g] * decay + mul(values, weights.astype(bf16))
            peak[g] = top

    for g in range(KVH):
        acc[g] = acc[g] * (1.0 / mass[g])
        peak[g] = peak[g] + jnp.log(mass[g])


def forward_kernel(held, query_ref, starts, low_out, flat_out, lse_out, acc, peak, mass):
    query = query_ref.at[0]
    rows = query.shape[1]
    run_forward(held, query, starts[0], own_block(), acc, peak, mass)
    for g in range(KVH):
        lse_out[0, g] = peak[g]
        for h in range(GROUP):
            head = g * GROUP + h
            flat_out[0, head * HD : (head + 1) * HD, :] = acc[g, :, h * rows : (h + 1) * rows]
    low_out[...] = flat_out[...].astype(bf16)


def one_of(dims, axis=0):
    block = tuple(1 if i == axis else n for i, n in enumerate(dims))
    return pl.BlockSpec(block, lambda m: tuple(m if i == axis else 0 for i in range(len(dims))))


def attend_forward(kv, query, starts):
    micro, width, rows = query.shape
    lanes = GROUP * rows
    low = shape_of(query.shape, bf16)
    flat = shape_of(query.shape, f32)
    lse = shape_of((micro, KVH, 1, lanes), f32)
    return pl.pallas_call(
        forward_kernel,
        grid=(micro,),
        in_specs=[one_of(kv.shape, 1), one_of(query.shape), one_of(starts.shape)],
        out_specs=[one_of(v.shape) for v in (low, flat, lse)],
        out_shape=[low, flat, lse],
        scratch_shapes=[
            pltpu.VMEM((KVH, HD, lanes), f32),
            pltpu.VMEM((KVH, 1, lanes), f32),
            pltpu.VMEM((KVH, 1, lanes), f32),
        ],
        compiler_params=params(),
        cost_estimate=cost(2.5),
        name="attention_forward",
    )(kv, query, starts)


def backward_kernel(
    held, q1_ref, q2_ref, d1_ref, d2_ref, o1, lse1, starts, far_starts, cos_ref, sin_ref,
    kv_out, first_grad, second_grad, sums, delta, dq, query2, both, acc, peak, mass,
):
    rows = q1_ref.shape[2]
    per = KEYS // rows
    query2[...] = (q2_ref[0] * FACTOR).astype(bf16)
    sums[...] = jnp.zeros_like(sums)
    dq[...] = jnp.zeros_like(dq)

    def attention(a, q_ref, d_ref, outs, lse, start, block_place):
        for g in range(KVH):
            query, grad = lane_heads(q_ref, g), lane_heads(d_ref, g)
            delta[a, g] = jnp.sum(grad.astype(f32) * outs(g), axis=0, keepdims=True)
            zero = jnp.zeros_like(query)
            both[g] = jnp.concatenate(
                [jnp.concatenate([query, zero], axis=1), jnp.concatenate([zero, grad], axis=1)], axis=0
            )

        @pl.loop(0, key_windows(start, block_place, rows))
        def _(step):
            first, block, bias = window(held, step, start, block_place, rows)
            tiles = [block[:, i * LANES : (i + 1) * LANES] for i in range(3)]
            total = []
            for g in range(KVH):
                pair = both[g]
                lanes = pair.shape[1] // 2
                products = mul(tiles[g], pair)
                weights = jnp.exp(products[:, :lanes] + bias - lse[g])
                score_grad = (weights * (products[:, lanes:] - delta[a, g])).astype(bf16)
                dq[a, g] += mul(jnp.transpose(tiles[g])[:HD], score_grad)
                total.append(mul_nt(jnp.concatenate([score_grad, weights.astype(bf16)], axis=1), pair))
            joined = jnp.concatenate(total, axis=1)
            sums[pl.ds(first, per)] += joined.reshape(per, rows, joined.shape[1])

    run_forward(held, query2, far_starts[0], far_block(), acc, peak, mass)
    attention(0, q1_ref.at[0], d1_ref.at[0], lambda g: lane_heads(o1.at[0], g), lse1.at[0], starts[0], own_block())
    attention(1, query2, d2_ref.at[0], lambda g: acc[g], peak, far_starts[0], far_block())
    kv_out[:, 0] = sums[...].astype(bf16)
    cosine, sine = cos_ref[...], -sin_ref[...]
    for g in range(KVH):
        for h in range(GROUP):
            head = g * GROUP + h
            lanes = slice(h * rows, (h + 1) * rows)
            target = slice(head * HD, (head + 1) * HD)
            parts = turn(dq[0, g][:, lanes] * FACTOR, cosine, sine, 1)
            first_grad[0, target, :] = jnp.concatenate(parts, axis=0).astype(bf16)
            second_grad[0, target, :] = (dq[1, g][:, lanes] * FACTOR).astype(bf16)


def attend_backward(kv, *arrays):
    micro, width, rows = arrays[0].shape
    lanes = GROUP * rows
    blocks, _, _, kv_width = kv.shape
    part = shape_of((micro, width, rows), bf16)
    table = pl.BlockSpec((HALF, rows), lambda m: (0, m))
    return pl.pallas_call(
        backward_kernel,
        grid=(micro,),
        in_specs=[one_of(kv.shape, 1)] + [one_of(v.shape) for v in arrays[:-2]] + [table] * 2,
        out_specs=[one_of(kv.shape, 1)] + [one_of(part.shape)] * 2,
        out_shape=[shape_of(kv.shape, bf16), part, part],
        scratch_shapes=[
            pltpu.VMEM((blocks, rows, kv_width), f32),
            pltpu.VMEM((2, KVH, 1, lanes), f32),
            pltpu.VMEM((2, KVH, HD, lanes), f32),
            pltpu.VMEM((width, rows), bf16),
            pltpu.VMEM((KVH, 2 * HD, 2 * lanes), bf16),
            pltpu.VMEM((KVH, HD, lanes), f32),
            pltpu.VMEM((KVH, 1, lanes), f32),
            pltpu.VMEM((KVH, 1, lanes), f32),
        ],
        compiler_params=params(),
        cost_estimate=cost(7),
        name="attention_backward",
    )(kv, *arrays)


def weights_kernel(
    sums, normed, starts, far_starts, own_normed, grad_ref, weight, wo_grad, gain_two_grad,
    normed_grad, kept, away, kv_out, packed,
):
    rows = starts.shape[2]
    width = weight.shape[0]
    per = KEYS // rows

    @pl.when(pl.program_id(0) == 0)
    def _():
        kv_out[...] = jnp.zeros_like(kv_out)

    def add(step):
        block = sums[pl.ds(step * per, per), 0].reshape(KEYS, sums.shape[3])
        inner = [normed[step * per + i, 0] for i in range(per)]
        values = jnp.concatenate([v[:width] for v in inner], axis=1)
        tables = jnp.concatenate([v[width:] for v in inner], axis=1).astype(f32)
        cosine = tables[:HALF] + tables[HALF : 2 * HALF]
        sine = tables[2 * HALF : 3 * HALF] + tables[3 * HALF :]
        flat = jnp.concatenate([jnp.transpose(block[:, g * LANES : (g + 1) * LANES]) for g in range(KVH)], axis=0)
        keys = turn(part_of(flat, 0).astype(f32), cosine, -sine, KVH)
        both = jnp.concatenate([jnp.concatenate(keys, axis=0).astype(bf16), part_of(flat, 1)], axis=0)
        kv_out[...] += mul_nt(both, values)

    near = key_steps(starts[0], own_block(), rows)
    far = key_steps(far_starts[0], far_block(), rows)
    pl.loop(*near)(add)

    @pl.loop(*far)
    def _(step):
        pl.when((step < near[0]) | (step >= near[1]))(lambda: add(step))


    @pl.when(pl.program_id(0) == pl.num_programs(0) - 1)
    def _():
        grad = side_by_side(grad_ref)
        values = jnp.concatenate([own_normed[m, :width] for m in range(own_normed.shape[0])], axis=1)
        normed_grad[...] = mul(weight[...], grad)
        lane = lax.broadcasted_iota(jnp.int32, (width, LANES), 1)
        gains = flip(jnp.where(lane == 0, gain_two_grad[...], 0.0))[:16]
        base = 0
        for array in (mul_nt(values, grad), kv_out[...], wo_grad[...], gains):
            base = pack_rows(packed, base, array.astype(bf16))
        packed[base:] = jnp.zeros((packed.shape[0] - base, LANES), bf16)
        unit = kept.shape[1]
        for dy in range(SIDE):
            for target, dc in ((kept, 0), (away, 1)):
                target[dy] = packed[pl.ds(pl.multiple_of(place_of(dc, dy, 1) * unit, 16), unit)]


def weights_back(sums, normed, starts, far_starts, *others):
    micro, _, rows = starts.shape
    width = others[2].shape[0]
    kv_width = sums.shape[3]
    unit = tail_rows(width)
    tail = shape_of((SIDE, unit, LANES), bf16)
    outs = [shape_of((width, micro * rows), f32), tail, tail]

    def whole(v):
        return pl.BlockSpec(v.shape, lambda m: (0,) * len(v.shape))

    return pl.pallas_call(
        weights_kernel,
        grid=(micro,),
        in_specs=[one_of(sums.shape, 1), one_of(normed.shape, 1), one_of(starts.shape), one_of(starts.shape)]
        + [whole(v) for v in others],
        out_specs=[whole(v) for v in outs],
        out_shape=outs,
        scratch_shapes=[
            pltpu.VMEM((kv_width, width), f32),
            pltpu.VMEM((2 * SIDE * unit, LANES), bf16),
        ],
        compiler_params=params(),
        cost_estimate=cost(3),
        name="weights_back",
    )(sums, normed, starts, far_starts, *others)


def norm_back(vector, scale, gain, gradient):
    weighted = gradient * gain
    gain_grad = jnp.sum(gradient * vector * scale, axis=1, keepdims=True)
    inner = jnp.mean(weighted * vector, axis=0, keepdims=True)
    return scale * weighted - vector * (scale * scale * scale * inner), gain_grad


def ffn_kernel(
    last, core, first, tokens, out_weight, gain, out_grad, wg, wu, wd, *refs,
):
    step = pl.program_id(0)
    micro, width, rows = tokens.shape
    if last:
        before, result_before, grad_before = refs[:3]
        result, main, middle_grad, d1, gain_grad, wo_grad = refs[3:9]
        normed, normed_t, grad, grad_t, result_sum, normed_grad = refs[9:]
        middle = before
    else:
        main, middle, result_sum, normed_grad = refs[:4]
        normed, normed_t, grad, grad_t = refs[4:]

    @pl.when(step == 0)
    def _():
        if last:
            value = before[...]
            result_sum[...] = result_before[...]
            normed_grad[...] = grad_before[...]
        else:
            value = side_by_side(tokens).astype(f32) + mul(flip(out_weight[...]), side_by_side(first))
            middle[...] = value
            result_sum[...] = jnp.zeros_like(result_sum)
            normed_grad[...] = jnp.zeros_like(normed_grad)
        scale = lax.rsqrt(jnp.mean(value * value, axis=0, keepdims=True) + EPSILON)
        low = (value * scale * gain[...].astype(f32)).astype(bf16)
        normed_t[...] = low
        normed[...] = flip(low)
        flat = side_by_side(out_grad)
        grad_t[...] = flat
        grad[...] = flip(flat)

    low = normed[...]
    gate = mul(low, wg[...])
    up = mul(low, wu[...])
    sigmoid = 1.0 / (1.0 + jnp.exp(-gate))
    active = gate * sigmoid
    hidden = (active * up).astype(bf16)
    result_sum[...] += mul_nt(hidden, wd[...])
    hidden_grad = mul(grad[...], wd[...])
    gate_grad = (hidden_grad * up * sigmoid * (1.0 + gate * (1.0 - sigmoid))).astype(bf16)
    up_grad = (hidden_grad * active).astype(bf16)
    parts = (mul(normed_t[...], gate_grad), mul(normed_t[...], up_grad), mul(grad_t[...], hidden))
    for i in range(CHUNK // LANES):
        span = slice(i * LANES, (i + 1) * LANES)
        for k, part in enumerate(parts):
            rows_at = slice((i * 3 + k) * width, (i * 3 + k + 1) * width)
            main[rows_at] = part[:, span].astype(bf16)
    normed_grad[...] += mul_nt(gate_grad, wg[...]) + mul_nt(up_grad, wu[...])
    if not last:
        return

    @pl.when(step == pl.num_programs(0) - 1)
    def _():
        value = middle[...]
        final = (value + flip(result_sum[...])).astype(bf16)
        scale = lax.rsqrt(jnp.mean(value * value, axis=0, keepdims=True) + EPSILON)
        part, gains = norm_back(value, scale, gain[...].astype(f32), flip(normed_grad[...]))
        gain_grad[...] = gains
        total = grad_t[...].astype(f32) + part
        middle_grad[...] = total
        branch = total.astype(bf16)
        wo_grad[...] = mul_nt(side_by_side(first), branch).astype(bf16)
        back = mul(out_weight[...], branch).astype(bf16)
        for m in range(micro):
            span = slice(m * rows, (m + 1) * rows)
            d1[m] = back[:, span]
            result[m] = final[:, span]


def pack_rows(target, base, array):
    rows, cols = array.shape
    for i in range(-(-cols // LANES)):
        span = array[:, i * LANES : (i + 1) * LANES]
        if span.shape[1] < LANES:
            span = jnp.concatenate([span, jnp.zeros((rows, LANES - span.shape[1]), span.dtype)], axis=1)
        target[base : base + rows] = span
        base += rows
    return base


def main_rows(width, hidden):
    used = hidden // 2 // LANES * 3 * width
    unit = SIDE * SIDE * SIDE * 8
    return -(-used // unit) * unit


def feed_forward(core, first, tokens, out_weight, gain, out_grad, wg, wu, wd, before):
    micro, width, rows = tokens.shape
    total = micro * rows
    hidden = wg.shape[1]
    steps = hidden // 2 // CHUNK
    block = pl.BlockSpec((CHUNK // LANES * 3 * width, LANES), lambda i, c: (i, 0))
    last = len(before) > 0

    def whole(*dims):
        return pl.BlockSpec(dims, lambda i, c: (0,) * len(dims))

    def column(i, c):
        side = c[0] if last else 1 - c[0]
        return (0, side * steps + i)

    weight = pl.BlockSpec((width, CHUNK), column)
    flat, natural = shape_of((width, total), f32), shape_of((total, width), f32)
    spec, tall = whole(width, total), whole(total, width)
    token_spec, token_shape = whole(micro, width, rows), shape_of((micro, width, rows), bf16)
    if last:
        outs = [
            (token_shape, token_spec),
            (shape_of((main_rows(width, hidden), LANES), bf16), block),
            (flat, spec),
            (token_shape, token_spec),
            (shape_of((width, 1), f32), whole(width, 1)),
            (shape_of((width, width), bf16), whole(width, width)),
        ]
        more = [spec, tall, tall]
        scratch = [pltpu.VMEM((total, width), f32)] * 2
    else:
        outs = [
            (shape_of((main_rows(width, hidden), LANES), bf16), block),
            (flat, spec),
            (natural, tall),
            (natural, tall),
        ]
        more, scratch = [], []
    low = [pltpu.VMEM((total, width), bf16), pltpu.VMEM((width, total), bf16)]
    return pl.pallas_call(
        functools.partial(ffn_kernel, last),
        grid_spec=pltpu.PrefetchScalarGridSpec(
            num_scalar_prefetch=1,
            grid=(steps,),
            in_specs=[
                token_spec,
                token_spec,
                whole(width, width),
                whole(width, 1),
                token_spec,
                weight,
                weight,
                weight,
            ]
            + more,
            out_specs=[v[1] for v in outs],
            scratch_shapes=low * 2 + scratch,
        ),
        out_shape=[v[0] for v in outs],
        compiler_params=params(),
        cost_estimate=cost(3),
        name="feed_forward",
    )(core, first, tokens, out_weight, gain, out_grad, wg, wu, wd, *before)


def tail_rows(width):
    tiles = -(-width // LANES)
    used = tiles * (2 * width + 2 * KVH * HD + 16)
    unit = 2 * SIDE * SIDE * SIDE * 8
    return -(-used // unit) * (unit // 2 // SIDE)


def place_of(dc, dy, sign):
    cc = lax.rem(lax.axis_index("core") + dc, 2)
    yy = lax.rem(lax.axis_index("y") + sign * dy + SIDE, SIDE)
    return cc * SIDE + yy


def input_back_kernel(
    kv_grad, wk, wv, cos_ref, sin_ref, partial, tokens, gain, middle_grad, second, input_grad, second_grad
):
    second_grad[...] = second[...]
    micro, width, rows = tokens.shape
    flat = jnp.concatenate(
        [flip(kv_grad[m * rows : (m + 1) * rows].astype(f32)) for m in range(micro)], axis=1
    )
    parts = turn(part_of(flat, 0), cos_ref[...], -sin_ref[...], KVH)
    low = jnp.concatenate(parts + [part_of(flat, 1)], axis=0).astype(bf16)
    weights = flip(jnp.concatenate([wk[...], wv[...]], axis=0))
    normed_grad = partial[...] + mul(weights, low)
    inputs = side_by_side(tokens).astype(f32)
    scale = lax.rsqrt(jnp.mean(inputs * inputs, axis=0, keepdims=True) + EPSILON)
    part, _ = norm_back(inputs, scale, gain[...].astype(f32), normed_grad)
    final = (middle_grad[...] + part).astype(bf16)
    for m in range(micro):
        input_grad[m] = final[:, m * rows : (m + 1) * rows]


def unpack_tail_kernel(kept, away, wq, wk, wv, gain, q_out, k_out, v_out, o_out, gain_one, gain_two, held):
    places, _, rows, _ = kept.shape
    for dy in range(SIDE):
        for source, dc in ((kept, 0), (away, 1)):
            base = place_of(dc, dy, -1) * places * rows
            for i in range(places):
                held[pl.ds(pl.multiple_of(base + i * rows, 16), rows)] = source[i, dy]
    width = q_out.shape[0]
    cut = k_out.shape[0]
    base = 0

    def section(rows, cols):
        nonlocal base
        count = -(-cols // LANES)
        parts = [held[base + i * rows : base + (i + 1) * rows] for i in range(count)]
        base += count * rows
        return jnp.concatenate(parts, axis=1)[:, :cols].astype(f32)

    query = section(width, width)
    both = section(2 * cut, width)
    key, value = both[:cut], both[cut:]
    q_out[...] = query
    k_out[...] = key
    v_out[...] = value
    o_out[...] = section(width, width)
    gain_two[...] = section(16, width)[0]
    total = jnp.sum(query * wq[...].astype(f32), axis=1, keepdims=True) / gain[...].astype(f32)
    total = flip(jnp.broadcast_to(total, (width, LANES)))[0:1]
    rest = jnp.sum(key * wk[...].astype(f32), axis=0, keepdims=True)
    rest = rest + jnp.sum(value * wv[...].astype(f32), axis=0, keepdims=True)
    line = flip(jnp.broadcast_to(gain[...].astype(f32), (width, LANES)))[0:1]
    gain_one[...] = (total + rest / line)[0]


def unpack_main_kernel(other, *refs):
    pieces = refs[: SIDE + 1]
    gate, up, down, held, wide, sems = refs[-6:]
    unit = pieces[0].shape[0]
    half = unit // 2
    for k, offset, piece in zip((0, 1, 2, 2, 3), (0, 0, 0, half, 0), pieces):
        place = lax.rem(lax.axis_index("y") - k + SIDE, SIDE)
        held[pl.ds(pl.multiple_of(place * unit + offset, 16), piece.shape[0])] = piece[...]
    core = lax.axis_index("core")
    core = 1 - core if other else core
    width, cols = wide.shape[1:]
    copies = []
    for k, target in enumerate((gate, up, down)):
        for t in range(cols // LANES):
            base = (t * 3 + k) * width
            wide[k, :, t * LANES : (t + 1) * LANES] = held[base : base + width].astype(f32)
        span = pl.ds(pl.multiple_of(core * cols, LANES), cols)
        copies.append(pltpu.make_async_copy(wide.at[k], target.at[:, span], sems.at[k]))
        copies[-1].start()
    for copy in copies:
        copy.wait()


def unpack_main(pieces, width, hidden, filled):
    unit = pieces[0].shape[0]
    outs = [shape_of((width, hidden), f32)] * 3
    return pl.pallas_call(
        functools.partial(unpack_main_kernel, filled is not None),
        in_specs=[VMEM] * len(pieces) + ([ANY] * 3 if filled else []),
        out_specs=[ANY] * 3,
        out_shape=outs,
        scratch_shapes=[
            pltpu.VMEM((SIDE * unit, LANES), bf16),
            pltpu.VMEM((3, width, hidden // 2), f32),
            pltpu.SemaphoreType.DMA((3,)),
        ],
        input_output_aliases={len(pieces) + i: i for i in range(3)} if filled else {},
        compiler_params=params(),
        cost_estimate=cost(1.5),
        name="unpack_main",
    )(*pieces, *(filled or ()))


def shift(value, axis, distance):
    size = lax.axis_size(axis)
    return lax.ppermute(value, axis, [(i, (i + distance) % size) for i in range(size)])


def mirror(value):
    size = SIDE * SIDE
    return lax.ppermute(value, SEQ, [(i, size - 1 - i) for i in range(size)])


def collect(value, axis):
    return [value] + [shift(value, axis, k) for k in range(1, SIDE)]


def exchange(parts, axis):
    total = parts[0].astype(f32)
    for k in range(1, SIDE):
        total = total + shift(parts[k], axis, k).astype(f32)
    return total


def scatter_parts(held, axis):
    rows, lanes = held.shape
    places = lax.axis_size(axis)
    return lax.all_to_all(held.reshape(places, rows // places, lanes), axis, 0, 0)


def sum_parts(parts):
    return jnp.sum(parts.astype(f32), axis=0).astype(bf16)


def scatter_sum(held, axis):
    return sum_parts(scatter_parts(held, axis))


def gather_all(held, axis):
    rows, lanes = held.shape
    places = lax.axis_size(axis)
    spread = jnp.broadcast_to(held[None], (places,) + held.shape)
    return lax.all_to_all(spread, axis, 0, 0).reshape(places * rows, lanes)


def after(value, *others):
    return lax.optimization_barrier((value, *others))[0]


def per_device(
    tokens,
    doc_lengths,
    second_query,
    second_grad,
    out_grad,
    first_gain,
    query_weight,
    key_weight,
    value_weight,
    output_weight,
    second_gain,
    gate_weight,
    up_weight,
    down_weight,
):
    micro, rows, width = tokens.shape
    kwidth = key_weight.shape[1]
    total = micro * rows
    tiles = -(-width // LANES)
    core = lax.axis_index("core").reshape(1)
    tokens, second_query, second_grad, out_grad = (
        jnp.swapaxes(v, 1, 2) for v in (tokens, second_query, second_grad, out_grad)
    )
    wk, wv, wd = key_weight.T, value_weight.T, down_weight.T
    gain_one, gain_two = first_gain.reshape(width, 1), second_gain.reshape(width, 1)

    table = shape_of((HALF, total), f32)
    start = shape_of((micro, 1, rows), jnp.int32)
    normed, kv, cosine, sine, starts, far_starts = simple(
        prepare_kernel,
        [SMEM] + [VMEM] * 4,
        [
            shape_of((micro, width + 4 * HALF, rows), bf16),
            shape_of((micro, rows, 2 * kwidth), bf16),
            table,
            table,
            start,
            start,
        ],
        (doc_lengths, tokens, first_gain, wk, wv),
        "prepare",
    )
    kv = lax.all_gather(kv, SEQ, axis=0)
    (q1,) = simple(
        query_kernel,
        [VMEM] * 4,
        [shape_of((micro, width, rows), bf16)],
        (normed, query_weight, cosine, sine),
        "query",
    )
    far_query, far_grad = mirror(second_query), mirror(second_grad)
    kv, q1, far_query, far_grad, gathered = lax.optimization_barrier((kv, q1, far_query, far_grad, normed))
    gathered = lax.all_gather(gathered, SEQ, axis=0)
    first_low, first_flat, first_lse = attend_forward(kv, q1, starts)
    ffn_args = (first_low, tokens, output_weight, gain_two, out_grad, gate_weight, up_weight, wd)
    away, *before = feed_forward(core, *ffn_args, ())
    result, main, middle_grad, d1, gain_two_grad, wo_grad = feed_forward(core, *ffn_args, before)
    main = (main.astype(f32) + shift(away, "core", 1).astype(f32)).astype(bf16)
    main = scatter_parts(main, "y")
    kv_grad, query_grad, second_query_grad = attend_backward(
        kv,
        q1,
        far_query,
        d1,
        far_grad,
        first_flat,
        first_lse,
        starts,
        far_starts,
        cosine,
        sine,
    )
    second_query_grad = mirror(second_query_grad)
    kv_grad, gathered, main = lax.optimization_barrier((kv_grad, gathered, main))
    main = scatter_parts(sum_parts(main), SEQ)
    normed_part, tail, tail_away = weights_back(
        kv_grad, gathered, starts, far_starts, normed, query_grad, query_weight, wo_grad, gain_two_grad
    )
    kv_grad = lax.psum_scatter(kv_grad.reshape(-1, 2 * kwidth), SEQ, scatter_dimension=0, tiled=True)
    tail_away, main = lax.optimization_barrier((tail_away, main))
    tail = (tail.astype(f32) + shift(tail_away, "core", 1).astype(f32)).astype(bf16)
    main = gather_all(sum_parts(main), SEQ)
    tail = exchange([tail[k] for k in range(SIDE)], "y").astype(bf16)
    tail, main, second_query_grad = lax.optimization_barrier((tail, main, second_query_grad))
    middle = main.shape[0] // 2
    ahead, behind = shift(main, "y", 1), shift(main, "y", -1)
    tokens_like = shape_of((micro, width, rows), bf16)
    input_grad, second_query_grad = simple(
        input_back_kernel,
        [VMEM] * 10,
        [tokens_like, tokens_like],
        (kv_grad, wk, wv, cosine, sine, normed_part, tokens, gain_one, middle_grad, second_query_grad),
        "input_back",
    )
    tail = scatter_sum(tail, SEQ)
    tail, ahead, behind = lax.optimization_barrier((tail, ahead, behind))
    tail = jnp.stack(collect(tail, "y"))
    places = SIDE * SIDE
    upper, lower = shift(ahead[:middle], "y", 1), shift(behind[middle:], "y", -1)
    tail, upper, lower = lax.optimization_barrier((tail, upper, lower))
    tail = lax.all_to_all(jnp.broadcast_to(tail[None], (places,) + tail.shape), SEQ, 0, 0)
    main = [main, ahead, upper, lower, behind]
    hidden = gate_weight.shape[1]
    main_away = [shift(v, "core", 1) for v in main]
    filled = unpack_main(main, width, hidden, None)
    gate, up, down = unpack_main(main_away, width, hidden, filled)
    tail, gate, up, down, input_grad, second_query_grad = lax.optimization_barrier(
        (tail, gate, up, down, input_grad, second_query_grad)
    )
    tail_away = shift(tail, "core", 1)
    square = shape_of((width, width), f32)
    narrow = shape_of((kwidth, width), f32)
    line = shape_of((width,), f32)
    q_total, k_total, v_total, o_total, gain_one_total, gain_two_total = pl.pallas_call(
        unpack_tail_kernel,
        in_specs=[VMEM] * 6,
        out_specs=[VMEM] * 6,
        out_shape=[square, narrow, narrow, square, line, line],
        scratch_shapes=[pltpu.VMEM((2 * math.prod(tail.shape[:3]), LANES), bf16)],
        compiler_params=params(),
        cost_estimate=cost(1),
        name="unpack_tail",
    )(tail, tail_away, query_weight, wk, wv, gain_one)
    return (
        jnp.swapaxes(result, 1, 2),
        jnp.swapaxes(input_grad, 1, 2),
        jnp.swapaxes(second_query_grad, 1, 2),
        gain_one_total,
        q_total,
        k_total.T,
        v_total.T,
        o_total,
        gain_two_total,
        gate,
        up,
        down.T,
    )


def exchange_all(value, axis):
    return [value.astype(f32)] + [shift(value, axis, k).astype(f32) for k in range(1, SIDE)]


def solution(mesh):
    grid = Mesh(mesh.devices.reshape(SIDE, SIDE, SIDE, 2), ("z", "x", "y", "core"))
    split = P(("y", "core"), SEQ, None)
    in_specs = (split, P(("y", "core"), None), split, split, split) + (P(),) * 9
    out_specs = (split, split, split) + (P(),) * 9
    return jax.shard_map(
        per_device, mesh=grid, in_specs=in_specs, out_specs=out_specs, check_vma=False
    )
```
